256 devices in a mesh: lat: 16 (over z, core), lon: 16 (over x, y).
Axes of the slice: x: 4, y: 4, z: 8, core: 2. Of those that a mesh axis runs over, the one named last changes fastest.
Arguments:
- fields: bfloat16 [6, 72, 512, 2048], P(None, None, 'lat', 'lon'), may hold values from -6 to 6
- frac_lat: float32 [72, 16, 512], P(None, 'lon', 'lat'), may hold values from 0 to 1
- off_lat: int32 [72, 16, 512], P(None, 'lon', 'lat'), may hold values from -7 to 6
- frac_lon: float32 [72, 16, 2048], P(None, 'lat', 'lon'), may hold values from 0 to 1
- off_lon: int32 [72, 16, 2048], P(None, 'lat', 'lon'), may hold values from -7 to 6
- sound_coef: float32 [72], replicated, may hold values from 0.5 to 2
- inverse: float32 [144, 144], replicated
Outputs:
- updated: bfloat16 [6, 72, 512, 2048], P(None, None, 'lat', 'lon')
The draws below stay inside these ranges and needn't reach their ends.
All inputs are finite; a program needn't handle non-finite values.
Results may differ from the reference program's by a relative error of at most 0.0065.
Values may be sent and summed in bfloat16 or wider, within the bound.
A program may use at most 128 MiB of HBM per device.

```python
import math
import jax
import jax.numpy as jnp
from jax import lax

LEV = 72
HALO = 8
TLAT = 32
TLON = 128
BANDS = 16
SECTORS = 16
NLAT = 512
NLON = 2048


def draw_off_lat(key, part):
    key = jax.random.fold_in(key, 11)
    values = jax.random.randint(key, (LEV, SECTORS, NLAT), 1 - HALO, HALO - 1, dtype=jnp.int32)
    return values.at[0, 0, 0].set(1 - HALO).at[0, 0, 1].set(HALO - 2)


def draw_off_lon(key, part):
    key = jax.random.fold_in(key, 23)
    values = jax.random.randint(key, (LEV, BANDS, NLON), 1 - HALO, HALO - 1, dtype=jnp.int32)
    return values.at[0, 0, 0].set(1 - HALO).at[0, 0, 1].set(HALO - 2)


def draw_inverse(key, part):
    key = jax.random.fold_in(key, 37)
    order = 2 * LEV
    noise = jax.random.normal(key, (order, order), jnp.float32)
    return jnp.eye(order, dtype=jnp.float32) + 0.5 * order ** (-0.5) * noise


def block_scale(own_key, shape, shards, low, high):
    level = 1.0
    for dim, shards_of in shards:
        steps = jax.random.uniform(jax.random.fold_in(jax.random.fold_in(own_key, 6), dim), (shards_of,), jnp.float32, low / len(shards), high / len(shards))
        level = level * jnp.repeat(jnp.exp(steps), shape[dim] // shards_of).reshape((-1,) + (1,) * (len(shape) - 1 - dim))
    return level


def centred(own_key, extent, scale, most, shards=(), kind=jnp.bfloat16):
    array = scale * jax.random.normal(own_key, extent, jnp.float32)
    if shards:
        array = array * block_scale(own_key, extent, shards, -0.22, 0.18)
    return jnp.clip(array, -most, most).astype(kind)


def setup_inputs(seed: int = 0) -> dict:
    key_of = jax.random.split(jax.random.key(seed), 8)
    fields = centred(key_of[0], (6, LEV, NLAT, NLON), 1.0, 6.0, ((2, 16), (3, 16)))
    frac_lat = jnp.clip(1.0 * jax.random.uniform(key_of[1], (LEV, SECTORS, NLAT), jnp.float32) ** block_scale(key_of[1], (LEV, SECTORS, NLAT), ((1, 16), (2, 16)), -0.2, 0.2), 0.0, 1.0)
    off_lat = draw_off_lat(jax.random.fold_in(key_of[7], 71), 0)
    frac_lon = jnp.clip(1.0 * jax.random.uniform(key_of[3], (LEV, BANDS, NLON), jnp.float32) ** block_scale(key_of[3], (LEV, BANDS, NLON), ((1, 16), (2, 16)), -0.2, 0.2), 0.0, 1.0)
    off_lon = draw_off_lon(jax.random.fold_in(key_of[7], 71), 0)
    sound_coef = jnp.clip(jnp.exp(jax.random.uniform(key_of[5], (LEV,), jnp.float32, math.log(0.5), math.log(2.0))), 0.5, 2.0)
    inverse = draw_inverse(jax.random.fold_in(key_of[7], 71), 0)
    return {"fields": fields, "frac_lat": frac_lat, "off_lat": off_lat, "frac_lon": frac_lon, "off_lon": off_lon, "sound_coef": sound_coef, "inverse": inverse}


def cubic_weights(fraction):
    return (-fraction * (fraction - 1.0) * (fraction - 2.0) / 6.0,
            (fraction + 1.0) * (fraction - 1.0) * (fraction - 2.0) / 2.0,
            -(fraction + 1.0) * fraction * (fraction - 2.0) / 2.0,
            (fraction + 1.0) * fraction * (fraction - 1.0) / 6.0)


def reference(fields, frac_lat, off_lat, frac_lon, off_lon, sound_coef, inverse):
    lat_weights = jnp.stack(cubic_weights(frac_lat)).astype(jnp.bfloat16)
    lon_weights = jnp.stack(cubic_weights(frac_lon)).astype(jnp.bfloat16)
    row_ids = jnp.arange(NLAT, dtype=jnp.int32)[:, None]
    col_ids = jnp.arange(NLON, dtype=jnp.int32)[None, :]

    def per_level(level):
        field_level = lax.dynamic_index_in_dim(fields, level, 1, keepdims=False)
        padded = jnp.pad(field_level, ((0, 0), (HALO, HALO), (0, 0)))
        flattened = padded.reshape(6, -1)
        lat_offs = jnp.repeat(off_lat[level].T, TLON, axis=1)
        lon_offs = jnp.repeat(off_lon[level], TLAT, axis=0)
        lat_gain = jnp.repeat(jnp.transpose(lat_weights[:, level], (0, 2, 1)), TLON, axis=2).astype(jnp.float32)
        lon_gain = jnp.repeat(lon_weights[:, level], TLAT, axis=1).astype(jnp.float32)
        summed = jnp.zeros((6, NLAT, NLON), jnp.float32)
        for lon_node in range(4):
            source_col = (col_ids + lon_offs + (lon_node - 1)) % NLON
            partial_sum = jnp.zeros((6, NLAT, NLON), jnp.float32)
            for lat_node in range(4):
                source_row = row_ids + lat_offs + (lat_node - 1 + HALO)
                flat_index = (source_row * NLON + source_col).astype(jnp.int32)
                picked = jnp.take(flattened, flat_index, axis=1).astype(jnp.float32)
                partial_sum = partial_sum + lat_gain[lat_node] * picked
            rounded = lax.optimization_barrier(partial_sum.astype(jnp.bfloat16))
            summed = summed + lon_gain[lon_node] * rounded.astype(jnp.float32)
        return summed.astype(jnp.bfloat16)

    departed = lax.map(per_level, jnp.arange(LEV, dtype=jnp.int32))
    east_west = departed[:, 0].astype(jnp.float32)
    north_south = jnp.pad(departed[:, 1].astype(jnp.float32), ((0, 0), (1, 1), (0, 0)))
    divergence = 0.5 * (jnp.roll(east_west, -1, axis=2) - jnp.roll(east_west, 1, axis=2))
    divergence = divergence + 0.5 * (north_south[:, 2:] - north_south[:, :-2])
    acoustic_rhs = jnp.concatenate([departed[:, 2].astype(jnp.float32),
                                    departed[:, 5].astype(jnp.float32) - sound_coef[:, None, None] * divergence], 0)
    corrected = jnp.dot(inverse, acoustic_rhs.reshape(2 * LEV, -1), precision=lax.Precision.HIGHEST,
                        preferred_element_type=jnp.float32).reshape(2 * LEV, NLAT, NLON).astype(jnp.bfloat16)
    return jnp.stack([departed[:, 0], departed[:, 1], corrected[:LEV], departed[:, 3], departed[:, 4], corrected[LEV:]], 0)
```

```python
import functools

import jax
import jax.numpy as jnp
from jax import lax
from jax.experimental import pallas as pl
from jax.experimental.pallas import tpu as pltpu
from jax.sharding import PartitionSpec as P

MESH = pl.DeviceIdType.MESH
HALO = 8
ROWS = 32
COLS = 128
GROUP = 8
FAR = -100000
OWNER = 1000
PAIRS = ((0, 1), (2, 5), (3, 4))
F32 = jnp.float32
BF16 = jnp.bfloat16


def cubic_weights(fraction):
    return (
        -fraction * (fraction - 1.0) * (fraction - 2.0) / 6.0,
        (fraction + 1.0) * (fraction - 1.0) * (fraction - 2.0) / 2.0,
        -(fraction + 1.0) * fraction * (fraction - 2.0) / 2.0,
        (fraction + 1.0) * fraction * (fraction - 1.0) / 6.0,
    )


def chunks_of(pair, groups):
    cuts, first = [], 0
    while first < groups:
        size = min(3, groups - first)
        if pair == len(PAIRS) - 1 and groups - first <= 3:
            size = 1
        cuts.append((first, size))
        first += size
    return cuts


def iota(shape, dim):
    return lax.broadcasted_iota(jnp.int32, shape, dim)


def taps(distance, weights):
    out = jnp.where(distance == 3, weights[3], 0.0)
    for node in (2, 1, 0):
        out = jnp.where(distance == node, weights[node], out)
    return out


def kernel(
    levels, bands, sectors,
    fields, frac_lat, off_lat, frac_lon, off_lon, sound, inverse, out,
    x, send_up, send_down, low, high, packed, send_right, send_left, from_left, from_right,
    send_corner, corner, merged, lat_w, lat_anchor, lat_matrix, lon_w, lon_anchor, lon_matrix,
    result, u, v, v_low, v_high, edge_right, edge_left, u_west, u_east, rhs, solved, acoustic,
    in_sem, out_sem, send_sem, recv_sem,
):
    groups = levels // GROUP
    doubles = (groups + 1) // 2
    a = lax.axis_index("lat")
    s = lax.axis_index("lon")
    up, down = lax.rem(a + 1, bands), lax.rem(a + bands - 1, bands)
    right, left = lax.rem(s + 1, sectors), lax.rem(s + sectors - 1, sectors)

    loads = [
        pltpu.make_async_copy(fields.at[f], x.at[f], in_sem.at[f]) for f in range(6)
    ]
    for pair in PAIRS:
        for f in pair:
            loads[f].start()

    barrier = pltpu.get_barrier_semaphore()
    for there in (
        (down, s), (up, s), (a, left), (a, right),
        (down, left), (down, right), (up, left), (up, right),
    ):
        pl.semaphore_signal(barrier, inc=1, device_id=there, device_id_type=MESH)

    sent = []

    def send(src, dst, there):
        k = len(sent)
        copy = pltpu.make_async_remote_copy(
            src_ref=src, dst_ref=dst, send_sem=send_sem.at[k], recv_sem=recv_sem.at[k],
            device_id=there, device_id_type=MESH,
        )
        copy.start()
        sent.append(copy)
        return copy

    def pack_rows(p):
        fa, fb = PAIRS[p]

        def body(g, carry):
            for q in range(GROUP):
                l = g * GROUP + q
                xa, xb = x[fa, l].astype(F32), x[fb, l].astype(F32)
                send_up[p, l] = jnp.concatenate([xa[24:32], xb[24:32]], 0).astype(BF16)
                send_down[p, l] = jnp.concatenate([xa[0:8], xb[0:8]], 0).astype(BF16)
            return carry

        lax.fori_loop(0, groups, body, 0)

    lane64 = iota((2 * ROWS, COLS), 1)
    even64 = (lane64 & 8) == 0

    def pack_columns(p):
        fa, fb = PAIRS[p]

        def body(g, carry):
            acc = jnp.zeros((2 * ROWS, COLS), F32)
            for q in range(GROUP):
                l = g * GROUP + q
                both = jnp.concatenate([x[fa, l], x[fb, l]], 0).astype(F32)
                turned = pltpu.roll(both, (8 + 16 * q) % COLS, 1)
                acc = jnp.where((lane64 >= 16 * q) & (lane64 < 16 * q + 16), turned, acc)
            packed[g] = acc
            return carry

        lax.fori_loop(0, groups, body, 0)
        if groups % 2:
            packed[groups] = jnp.zeros((2 * ROWS, COLS), F32)

        def merge(d, carry):
            first, second = packed[2 * d], packed[2 * d + 1]
            to_right = jnp.where(even64, first, pltpu.roll(second, 8, 1))
            to_left = jnp.where(even64, pltpu.roll(second, COLS - 8, 1), first)
            send_right[p, d] = to_right.astype(BF16)
            send_left[p, d] = to_left.astype(BF16)
            for c, (block, row) in enumerate(
                ((to_left, 0), (to_right, 0), (to_left, 24), (to_right, 24))
            ):
                send_corner[c, p, d] = jnp.concatenate(
                    [block[row : row + 8], block[row + 32 : row + 40]], 0
                ).astype(BF16)
            return carry

        lax.fori_loop(0, doubles, merge, 0)

    lat_copies, lon_copies = {}, {}
    for p, (fa, fb) in enumerate(PAIRS):
        loads[fa].wait()
        loads[fb].wait()
        pack_rows(p)
        if p == 0:
            pl.semaphore_wait(barrier, 8)
        for k, (first, size) in enumerate(chunks_of(p, groups)):
            span = pl.ds(first * GROUP, size * GROUP)
            lat_copies[p, k] = (
                send(send_up.at[p, span], low.at[p, span], (up, s)),
                send(send_down.at[p, span], high.at[p, span], (down, s)),
            )
            if k == 0:
                pack_columns(p)
                lon_copies[p] = [
                    send(send_right.at[p], from_left.at[p], (a, right)),
                    send(send_left.at[p], from_right.at[p], (a, left)),
                ]
                for c, there in enumerate(
                    ((down, left), (down, right), (up, left), (up, right))
                ):
                    lon_copies[p].append(send(send_corner.at[c, p], corner.at[c, p], there))

    lane_row = iota(lat_anchor.shape, 1)
    rounded = [w.astype(BF16).astype(F32) for w in cubic_weights(frac_lat[...])]
    for node in range(4):
        lat_w[node] = rounded[node]
    lat_anchor[...] = off_lat[...] + (lane_row & 31) + (HALO - 1) + ((lane_row & 32) >> 5) * OWNER
    rounded = [w.astype(BF16).astype(F32) for w in cubic_weights(frac_lon[...])]
    for node in range(4):
        lon_w[node] = rounded[node]
    lon_anchor[...] = off_lon[...] + iota(lon_anchor.shape, 1) + (HALO - 1)

    r = iota((96, COLS), 0)
    own = jnp.where(r < 32, r + HALO, r - 32 + HALO + OWNER)
    below = jnp.where(r < 72, r - 64, r - 72 + OWNER)
    above = jnp.where(r < 88, r - 80 + HALO + ROWS, r - 88 + HALO + ROWS + OWNER)
    below = jnp.where(a == 0, FAR, below)
    above = jnp.where(a == bands - 1, FAR, above)
    row_place = jnp.where(r < 64, own, jnp.where(r < 80, below, above))

    def build_lat(j, carry):
        distance = row_place - lat_anchor[pl.ds(j, 1), :]
        turned = taps(distance, [lat_w[node, pl.ds(j, 1), :] for node in range(4)]).T.astype(BF16)
        lat_matrix[2 * j] = turned[0:64]
        lat_matrix[2 * j + 1] = turned[64:128]
        return carry

    lax.fori_loop(0, levels // 2, build_lat, 0)

    place = iota((COLS, COLS), 0) + HALO
    r16 = iota((16, COLS), 0)
    left_first = jnp.where(r16 < 8, r16, r16 - 8 + HALO + COLS)
    right_first = jnp.where(r16 < 8, r16 + HALO + COLS, r16 - 8)

    def build_lon(g, carry):
        edge_place = jnp.where((g & 1) == 0, left_first, right_first)
        for q in range(GROUP):
            l = g * GROUP + q
            anchor = lon_anchor[pl.ds(l, 1), :]
            weights = [lon_w[node, pl.ds(l, 1), :] for node in range(4)]
            lon_matrix[l, 0:COLS] = taps(place - anchor, weights).astype(BF16)
            lon_matrix[l, COLS:] = jnp.zeros((COLS, COLS), BF16)
            lon_matrix[l, COLS + 16 * q : COLS + 16 * q + 16] = taps(
                edge_place - anchor, weights
            ).astype(BF16)
        return carry

    lax.fori_loop(0, groups, build_lon, 0)

    inv = inverse[...]
    acoustic[...] = jnp.concatenate([inv, -(inv[:, levels:] * sound[...])], 1).astype(BF16)

    even16 = (iota((16, COLS), 1) & 8) == 0

    def merge_halo(p):
        def body(d, carry):
            l_in, r_in = from_left[p, d].astype(F32), from_right[p, d].astype(F32)
            merged[p, 2 * d, 0:64] = jnp.where(even64, l_in, r_in).astype(BF16)
            merged[p, 2 * d + 1, 0:64] = jnp.where(even64, r_in, l_in).astype(BF16)
            for n, (cl, cr) in enumerate(((3, 2), (1, 0))):
                l_in, r_in = corner[cl, p, d].astype(F32), corner[cr, p, d].astype(F32)
                row = 64 + 16 * n
                merged[p, 2 * d, row : row + 16] = jnp.where(even16, l_in, r_in).astype(BF16)
                merged[p, 2 * d + 1, row : row + 16] = jnp.where(even16, r_in, l_in).astype(BF16)
            return carry

        lax.fori_loop(0, doubles, body, 0)

    writes = []

    def write(f, first, size):
        k = len(writes)
        span = pl.ds(first * GROUP, size * GROUP)
        copy = pltpu.make_async_copy(result.at[f, span], out.at[f, span], out_sem.at[k])
        copy.start()
        writes.append(copy)

    def interpolate(p):
        fa, fb = PAIRS[p]
        for k, (first, size) in enumerate(chunks_of(p, groups)):
            for copy in lat_copies[p, k]:
                copy.wait_recv()
            if k == 0:
                for copy in lon_copies[p]:
                    copy.wait_recv()
                merge_halo(p)

            def body(g, carry):
                halo = merged[p, g]
                for q in range(GROUP):
                    l = g * GROUP + q
                    main = jnp.concatenate([x[fa, l], x[fb, l], low[p, l], high[p, l]], 0)
                    y = jnp.dot(
                        lat_matrix[l], jnp.concatenate([main, halo], 1), preferred_element_type=F32
                    ).astype(BF16)
                    z = jnp.dot(y, lon_matrix[l], preferred_element_type=F32).astype(BF16)
                    if p != 1:
                        result[fa, l] = z[0:ROWS]
                        result[fb, l] = z[ROWS:]
                    if p < 2:
                        wide = z.astype(F32)
                        for i in range(0, ROWS, 8):
                            one, two = wide[i : i + 8], wide[ROWS + i : ROWS + i + 8]
                            if p == 0:
                                u[pl.ds(i * levels + l, 8, stride=levels), :] = one
                                v[pl.ds(i * levels + l, 8, stride=levels), :] = two
                            else:
                                at = i * 3 * levels + l
                                rhs[pl.ds(at, 8, stride=3 * levels), :] = one
                                rhs[pl.ds(at + levels, 8, stride=3 * levels), :] = two
                return carry

            lax.fori_loop(first, first + size, body, 0)
            if p != 1:
                write(fa, first, size)
                write(fb, first, size)

    lane = iota((levels, COLS), 1)
    interpolate(0)

    def pack_edges(i, carry):
        block = u[pl.ds(pl.multiple_of(i * levels, 8), levels), :]
        to_right, to_left = carry
        here = lane == i
        return (
            jnp.where(here, pltpu.roll(block, i + 1, 1), to_right),
            jnp.where(here, pltpu.roll(block, i, 1), to_left),
        )

    nothing = jnp.zeros((levels, COLS), F32)
    to_right, to_left = lax.fori_loop(0, ROWS, pack_edges, (nothing, nothing))
    edge_right[...] = to_right
    edge_left[...] = to_left
    edges = [
        send(edge_right, u_west, (a, right)),
        send(edge_left, u_east, (a, left)),
        send(v.at[pl.ds((ROWS - 1) * levels, levels)], v_low, (up, s)),
        send(v.at[pl.ds(0, levels)], v_high, (down, s)),
    ]

    interpolate(1)
    for copy in edges:
        copy.wait_recv()

    v_low[...] = jnp.where(a == 0, 0.0, v_low[...])
    v_high[...] = jnp.where(a == bands - 1, 0.0, v_high[...])

    def diverge(i, south, north):
        block = u[pl.ds(pl.multiple_of(i * levels, 8), levels), :]
        back = lax.rem(COLS - i, COLS)
        west = jnp.where(lane == 0, pltpu.roll(u_west[...], back, 1), pltpu.roll(block, 1, 1))
        east = jnp.where(
            lane == COLS - 1,
            pltpu.roll(u_east[...], COLS - 1 - i, 1),
            pltpu.roll(block, COLS - 1, 1),
        )
        at = pl.multiple_of(i * 3 * levels + 2 * levels, 8)
        rhs[pl.ds(at, levels), :] = 0.5 * (east - west) + 0.5 * (north - south)

    def v_row(i):
        return v[pl.ds(pl.multiple_of(i * levels, 8), levels), :]

    diverge(0, v_low[...], v_row(1))

    def inner(i, carry):
        diverge(i, v_row(i - 1), v_row(i + 1))
        return carry

    lax.fori_loop(1, ROWS - 1, inner, 0)
    diverge(ROWS - 1, v_row(ROWS - 2), v_high[...])

    def solve(h, carry):
        at = pl.multiple_of(2 * h * 3 * levels, 8)
        both = jnp.concatenate(
            [rhs[pl.ds(at, 3 * levels), :], rhs[pl.ds(at + 3 * levels, 3 * levels), :]], 1
        ).astype(BF16)
        answer = jnp.dot(acoustic[...], both, preferred_element_type=F32)
        for c in range(0, 2 * levels, 8):
            solved[pl.ds(c * ROWS + 2 * h, 8, stride=ROWS), :] = answer[c : c + 8, :COLS]
            solved[pl.ds(c * ROWS + 2 * h + 1, 8, stride=ROWS), :] = answer[c : c + 8, COLS:]
        return carry

    lax.fori_loop(0, ROWS // 2, solve, 0)

    def round_off(g, carry):
        for q in range(GROUP):
            l = g * GROUP + q
            result[2, l] = solved[pl.ds(pl.multiple_of(l * ROWS, ROWS), ROWS), :].astype(BF16)
            result[5, l] = solved[
                pl.ds(pl.multiple_of((l + levels) * ROWS, ROWS), ROWS), :
            ].astype(BF16)
        return carry

    lax.fori_loop(0, groups, round_off, 0)
    write(2, 0, groups)
    write(5, 0, groups)

    interpolate(2)
    for copy in sent:
        copy.wait_send()
    for copy in writes:
        copy.wait()


def local(bands, sectors, fields, frac_lat, off_lat, frac_lon, off_lon, sound_coef, inverse):
    levels = fields.shape[1]
    groups = levels // GROUP
    doubles = (groups + 1) // 2

    def twice(block):
        block = block[:, 0, :]
        return jnp.concatenate([block, block], 1).reshape(levels // 2, COLS)

    vmem = pl.BlockSpec(memory_space=pltpu.VMEM)
    anywhere = pl.BlockSpec(memory_space=pl.ANY)
    halo_rows = pltpu.VMEM((3, levels, 16, COLS), BF16)
    halo_columns = pltpu.VMEM((3, doubles, 2 * ROWS, COLS), BF16)
    corners = pltpu.VMEM((4, 3, doubles, 16, COLS), BF16)
    level_rows = pltpu.VMEM((levels, COLS), F32)
    whole = pltpu.VMEM((ROWS * levels, COLS), F32)
    messages = 2 * sum(len(chunks_of(p, groups)) for p in range(3)) + 18 + 4
    outgoing = 2 * len(chunks_of(0, groups)) + 2 * len(chunks_of(2, groups)) + 2
    return pl.pallas_call(
        functools.partial(kernel, levels, bands, sectors),
        out_shape=jax.ShapeDtypeStruct(fields.shape, BF16),
        in_specs=[anywhere] + [vmem] * 6,
        out_specs=anywhere,
        scratch_shapes=[
            pltpu.VMEM(fields.shape, BF16),
            halo_rows, halo_rows, halo_rows, halo_rows,
            pltpu.VMEM((2 * doubles, 2 * ROWS, COLS), F32),
            halo_columns, halo_columns, halo_columns, halo_columns,
            corners, corners,
            pltpu.VMEM((3, 2 * doubles, 96, COLS), BF16),
            pltpu.VMEM((4, levels // 2, COLS), F32),
            pltpu.VMEM((levels // 2, COLS), jnp.int32),
            pltpu.VMEM((levels, 64, 96), BF16),
            pltpu.VMEM((4, levels, COLS), F32),
            pltpu.VMEM((levels, COLS), jnp.int32),
            pltpu.VMEM((levels, 2 * COLS, COLS), BF16),
            pltpu.VMEM(fields.shape, BF16),
            whole, whole,
            level_rows, level_rows, level_rows, level_rows, level_rows, level_rows,
            pltpu.VMEM((3 * ROWS * levels, COLS), F32),
            pltpu.VMEM((2 * ROWS * levels, COLS), F32),
            pltpu.VMEM((2 * levels, 3 * levels), BF16),
            pltpu.SemaphoreType.DMA((6,)),
            pltpu.SemaphoreType.DMA((outgoing,)),
            pltpu.SemaphoreType.DMA((messages,)),
            pltpu.SemaphoreType.DMA((messages,)),
        ],
        compiler_params=pltpu.CompilerParams(
            collective_id=0, has_side_effects=True, vmem_limit_bytes=48 * 2**20
        ),
        cost_estimate=pl.CostEstimate(
            flops=10**9, bytes_accessed=2 * 2 * fields.size, transcendentals=0
        ),
    )(
        fields, twice(frac_lat), twice(off_lat), frac_lon[:, 0, :], off_lon[:, 0, :],
        sound_coef[None, :], inverse,
    )


def solution(mesh):
    placed = (
        P(None, None, "lat", "lon"),
        P(None, "lon", "lat"),
        P(None, "lon", "lat"),
        P(None, "lat", "lon"),
        P(None, "lat", "lon"),
        P(),
        P(),
    )
    return jax.shard_map(
        functools.partial(local, mesh.shape["lat"], mesh.shape["lon"]),
        mesh=mesh, in_specs=placed, out_specs=P(None, None, "lat", "lon"), check_vma=False,
    )
```

```python
import functools

import jax
import jax.numpy as jnp
from jax import lax
from jax.experimental import pallas as pl
from jax.experimental.pallas import tpu as pltpu
from jax.sharding import PartitionSpec as P

MESH = pl.DeviceIdType.MESH
HALO = 8
ROWS = 32
COLS = 128
GROUP = 8
FAR = -100000
PAIRS = ((0, 1), (2, 5), (3, 4))
F32 = jnp.float32
BF16 = jnp.bfloat16
LON = BF16
PIECES = 2


def cubic_weights(fraction):
    return (
        -fraction * (fraction - 1.0) * (fraction - 2.0) / 6.0,
        (fraction + 1.0) * (fraction - 1.0) * (fraction - 2.0) / 2.0,
        -(fraction + 1.0) * fraction * (fraction - 2.0) / 2.0,
        (fraction + 1.0) * fraction * (fraction - 1.0) / 6.0,
    )


def chunks_of(pair, groups):
    cuts, first = [], 0
    while first < groups:
        size = min(3, groups - first)
        if pair == len(PAIRS) - 1 and groups - first <= 3:
            size = 1
        cuts.append((first, size))
        first += size
    return cuts


def iota(shape, dim):
    return lax.broadcasted_iota(jnp.int32, shape, dim)


def taps(distance, weights):
    out = jnp.where(distance == 3, weights[3], jnp.zeros((), weights[3].dtype))
    for node in (2, 1, 0):
        out = jnp.where(distance == node, weights[node], out)
    return out


def kernel(
    levels, bands, sectors,
    fields, frac_lat, off_lat, frac_lon, off_lon, sound, inverse, final,
    out, x, frac_lat_in, off_lat_in, frac_lon_in, off_lon_in, sound_in, inverse_in,
    frac_lat_t, off_lat_t,
    send_up, send_down, low, high, picker, packed, send_right, send_left, from_left, from_right,
    send_corner, corner, merged, lat_w, lat_anchor, lat_matrix, lon_w, lon_anchor, lon_matrix,
    interim, u, v, v_first, v_last, v_low, v_high, edge_right, edge_left, u_west, u_east, u_edges,
    rhs, solved, acoustic, slope,
    in_sem, out_sem, send_sem, recv_sem,
):
    groups = levels // GROUP
    doubles = (groups + 1) // 2
    u_step, rhs_step, solved_step = levels + 1, 3 * levels + 1, ROWS + 1
    a = lax.axis_index("lat")
    s = lax.axis_index("lon")
    up, down = lax.rem(a + 1, bands), lax.rem(a + bands - 1, bands)
    right, left = lax.rem(s + 1, sectors), lax.rem(s + sectors - 1, sectors)

    started = []

    def load(src, dst):
        copy = pltpu.make_async_copy(src, dst, in_sem.at[len(started)])
        copy.start()
        started.append(copy)
        return copy

    loads = {}
    for p, pair in enumerate(PAIRS):
        for k, (first, size) in enumerate(chunks_of(p, groups) if p == 0 else [(0, groups)]):
            span = pl.ds(first * GROUP, size * GROUP)
            loads[p, k] = [load(fields.at[f, span], x.at[f, span]) for f in pair]
    small = [
        load(src, dst)
        for src, dst in (
            (frac_lon.at[:, 0, :], frac_lon_in), (off_lon.at[:, 0, :], off_lon_in),
            (frac_lat, frac_lat_in), (off_lat, off_lat_in),
            (sound, sound_in), (inverse, inverse_in),
        )
    ]

    barrier = pltpu.get_barrier_semaphore()
    for there in (
        (down, s), (up, s), (a, left), (a, right),
        (down, left), (down, right), (up, left), (up, right),
    ):
        pl.semaphore_signal(barrier, inc=1, device_id=there, device_id_type=MESH)

    sent = []

    def send(src, dst, there):
        k = len(sent)
        copy = pltpu.make_async_remote_copy(
            src_ref=src, dst_ref=dst, send_sem=send_sem.at[k], recv_sem=recv_sem.at[k],
            device_id=there, device_id_type=MESH,
        )
        copy.start()
        sent.append(copy)
        return copy

    def pack_rows(p, first, size):
        fa, fb = PAIRS[p]

        def rows_body(g, carry):
            for q in range(GROUP):
                l = g * GROUP + q
                xa, xb = x[fa, l].astype(F32), x[fb, l].astype(F32)
                send_up[p, l] = jnp.concatenate([xa[24:32], xb[24:32]], 0).astype(BF16)
                send_down[p, l] = jnp.concatenate([xa[0:8], xb[0:8]], 0).astype(BF16)
            return carry

        lax.fori_loop(first, first + size, rows_body, 0)

    def build_picker(t, carry):
        k = iota((2 * COLS, COLS), 0)
        column = k & (COLS - 1)
        q = 2 * t + jnp.where(k >= COLS, 1, 0)
        slot = 16 * (q & 7)
        second = q & 8
        target = jnp.where(
            column >= COLS - HALO,
            slot + second + column - (COLS - HALO),
            jnp.where(column < HALO, COLS + slot + (8 - second) + column, -1),
        )
        lane = iota((2 * COLS, COLS), 1)
        picker[t, :, 0:COLS] = jnp.where(target == lane, 1.0, 0.0).astype(BF16)
        picker[t, :, COLS:] = jnp.where(target == lane + COLS, 1.0, 0.0).astype(BF16)
        return carry

    lax.fori_loop(0, 8, build_picker, 0)

    def pack_columns(pairs):
        for t in range(8):
            rows = []
            for p in pairs:
                for d in range(doubles):
                    l = 16 * d + 2 * t
                    if l < levels:
                        for f in PAIRS[p]:
                            rows.append(jnp.concatenate([x[f, l], x[f, l + 1]], 1))
            part = jnp.dot(jnp.concatenate(rows, 0), picker[t], preferred_element_type=F32)
            at = 0
            for p in pairs:
                for d in range(doubles):
                    if 16 * d + 2 * t < levels:
                        block = part[at : at + 2 * ROWS]
                        at += 2 * ROWS
                        packed[p, d] = block if t == 0 else packed[p, d] + block
        for p in pairs:

            def merge(d, carry):
                block = packed[p, d]
                to_right, to_left = block[:, :COLS], block[:, COLS:]
                send_right[p, d] = to_right.astype(BF16)
                send_left[p, d] = to_left.astype(BF16)
                for c, (side, row) in enumerate(
                    ((to_left, 0), (to_right, 0), (to_left, 24), (to_right, 24))
                ):
                    send_corner[c, p, d] = jnp.concatenate(
                        [side[row : row + 8], side[row + 32 : row + 40]], 0
                    ).astype(BF16)
                return carry

            lax.fori_loop(0, doubles, merge, 0)

    lat_copies, lon_copies = {}, {}

    def send_rows(p, k, first, size):
        span = pl.ds(first * GROUP, size * GROUP)
        lat_copies[p, k] = (
            send(send_up.at[p, span], low.at[p, span], (up, s)),
            send(send_down.at[p, span], high.at[p, span], (down, s)),
        )

    def send_columns(p):
        lon_copies[p] = [
            send(send_corner.at[c, p], corner.at[c, p], there)
            for c, there in enumerate(((down, left), (down, right), (up, left), (up, right)))
        ]
        lon_copies[p].append(send(send_right.at[p], from_left.at[p], (a, right)))
        lon_copies[p].append(send(send_left.at[p], from_right.at[p], (a, left)))

    for k, (first, size) in enumerate(chunks_of(0, groups)):
        for copy in loads[0, k]:
            copy.wait()
        pack_rows(0, first, size)
        if k == 0:
            pl.semaphore_wait(barrier, 8)
        send_rows(0, k, first, size)
    pack_columns([0])
    send_columns(0)
    for p in (1, 2):
        for copy in loads[p, 0]:
            copy.wait()
        pack_rows(p, 0, groups)
    pack_columns([1, 2])
    for k, (first, size) in enumerate(chunks_of(1, groups)):
        send_rows(1, k, first, size)
    send_columns(1)
    send_columns(2)
    for copy in small:
        copy.wait()

    rounded = [w.astype(BF16).astype(F32) for w in cubic_weights(frac_lon_in[...])]
    for node in range(4):
        lon_w[node] = rounded[node]
    lon_anchor[...] = (off_lon_in[...] + iota(lon_anchor.shape, 1) + (HALO - 1)).astype(F32)

    place = (iota((COLS, COLS), 0) + HALO).astype(F32).astype(LON)
    r16 = iota((16, COLS), 0)
    left_first = jnp.where(r16 < 8, r16, r16 - 8 + HALO + COLS).astype(F32)
    right_first = jnp.where(r16 < 8, r16 + HALO + COLS, r16 - 8).astype(F32)

    def build_lon(g, carry):
        edge_place = jnp.where((g & 1) == 0, left_first, right_first).astype(LON)
        for q in range(GROUP):
            l = g * GROUP + q
            anchor = jnp.broadcast_to(lon_anchor[pl.ds(l, 1), :], (16, COLS)).astype(LON)
            weights = [
                jnp.broadcast_to(lon_w[node, pl.ds(l, 1), :], (16, COLS)).astype(LON)
                for node in range(4)
            ]
            for t in range(0, COLS, 16):
                lon_matrix[l, t : t + 16] = taps(place[t : t + 16] - anchor, weights).astype(BF16)
            lon_matrix[l, COLS:] = jnp.zeros((COLS, COLS), BF16)
            lon_matrix[l, COLS + 16 * q : COLS + 16 * q + 16] = taps(
                edge_place - anchor, weights
            ).astype(BF16)
        return carry

    lax.fori_loop(0, groups, build_lon, 0)

    frac_lat_t[...] = frac_lat_in[...].T
    off_lat_t[...] = off_lat_in[...].T
    quarter = levels // 4
    lane_row = iota((quarter, COLS), 1)

    def side_by_side(ref):
        total = None
        for q in range(4):
            part = ref[pl.ds(q, quarter, stride=4), :]
            part = jnp.concatenate([part] * 4, 1)
            total = part if total is None else jnp.where(lane_row >= ROWS * q, part, total)
        return total

    rounded = [w.astype(BF16).astype(F32) for w in cubic_weights(side_by_side(frac_lat_t))]
    for node in range(4):
        lat_w[node] = rounded[node]
    lat_anchor[...] = side_by_side(off_lat_t) + (lane_row & (ROWS - 1)) + (HALO - 1)

    r = iota((ROWS + 2 * HALO, COLS), 0)
    below = jnp.where(a == 0, FAR, r - ROWS)
    above = jnp.where(a == bands - 1, FAR, r)
    row_place = jnp.where(r < ROWS, r + HALO, jnp.where(r < ROWS + HALO, below, above))

    def build_lat(h, carry):
        turned = []
        for n in range(3):
            j = 3 * h + n
            distance = row_place - lat_anchor[pl.ds(j, 1), :]
            weights = [lat_w[node, pl.ds(j, 1), :] for node in range(4)]
            turned.append(taps(distance, weights).astype(BF16).T)
        for n in range(3):
            for q in range(4):
                lat_matrix[4 * (3 * h + n) + q] = turned[n][ROWS * q : ROWS * q + ROWS]
        return carry

    lax.fori_loop(0, quarter // 3, build_lat, 0)

    inv = inverse_in[...]
    acoustic[...] = jnp.concatenate([inv, -(inv[:, levels:] * sound_in[...])], 1).astype(BF16)
    k, j = iota(slope.shape, 0), iota(slope.shape, 1)
    minus = ((k < COLS) & (k == j - 1)) | ((k >= COLS) & (k < COLS + ROWS) & (j == 0))
    plus = ((k < COLS) & (k == j + 1)) | (
        (k >= COLS + ROWS) & (k < COLS + 2 * ROWS) & (j == COLS - 1)
    )
    slope[...] = jnp.where(plus, 0.5, jnp.where(minus, -0.5, 0.0)).astype(BF16)

    even64 = (iota((2 * ROWS, COLS), 1) & 8) == 0
    even16 = (iota((16, COLS), 1) & 8) == 0

    def merge_halo(p):
        def halo_body(d, carry):
            l_in, r_in = from_left[p, d].astype(F32), from_right[p, d].astype(F32)
            mine = jnp.where(even64, l_in, r_in), jnp.where(even64, r_in, l_in)
            low_l, low_r = corner[3, p, d].astype(F32), corner[2, p, d].astype(F32)
            high_l, high_r = corner[1, p, d].astype(F32), corner[0, p, d].astype(F32)
            lows = jnp.where(even16, low_l, low_r), jnp.where(even16, low_r, low_l)
            highs = jnp.where(even16, high_l, high_r), jnp.where(even16, high_r, high_l)
            for n in range(2):
                for f in range(2):
                    merged[p, 2 * d + n, f] = jnp.concatenate(
                        [
                            mine[n][ROWS * f : ROWS * f + ROWS],
                            lows[n][8 * f : 8 * f + 8],
                            highs[n][8 * f : 8 * f + 8],
                        ],
                        0,
                    ).astype(BF16)
            return carry

        lax.fori_loop(0, doubles, halo_body, 0)

    def along_lat(p, g):
        fa, fb = PAIRS[p]
        for q in range(GROUP):
            l = g * GROUP + q
            below, above = low[p, l].astype(F32), high[p, l].astype(F32)
            around = [
                jnp.concatenate([below[n : n + 8], above[n : n + 8]], 0).astype(BF16)
                for n in (0, 8)
            ]
            block = jnp.concatenate(
                [
                    jnp.concatenate([x[fa, l], around[0]], 0),
                    merged[p, g, 0],
                    jnp.concatenate([x[fb, l], around[1]], 0),
                    merged[p, g, 1],
                ],
                1,
            )
            y = jnp.dot(lat_matrix[l], block, preferred_element_type=F32).astype(BF16)
            interim[q] = jnp.concatenate([y[:, : 2 * COLS], y[:, 2 * COLS :]], 0)

    def along_lon(p, g):
        fa, fb = PAIRS[p]
        for q in range(GROUP):
            l = g * GROUP + q
            z = jnp.dot(interim[q], lon_matrix[l], preferred_element_type=F32).astype(BF16)
            one, two = z[:ROWS], z[ROWS:]
            if p != 1:
                out[fa, l] = one
                out[fb, l] = two
            if p < 2:
                one, two = one.astype(F32), two.astype(F32)
                for i in range(0, ROWS, 8):
                    if p == 0:
                        u[pl.ds(i * u_step + l, 8, stride=u_step), :] = one[i : i + 8]
                        v[pl.ds((i + 1) * u_step + l, 8, stride=u_step), :] = two[i : i + 8]
                    else:
                        at = i * rhs_step + l
                        rhs[pl.ds(at, 8, stride=rhs_step), :] = one[i : i + 8]
                        rhs[pl.ds(at + levels, 8, stride=rhs_step), :] = two[i : i + 8]

    writes = []

    def write(f, first, size):
        span = pl.ds(first * GROUP, size * GROUP)
        copy = pltpu.make_async_copy(out.at[f, span], final.at[f, span], out_sem.at[len(writes)])
        copy.start()
        writes.append(copy)

    def interpolate(p, chunks):
        for k in chunks:
            first, size = chunks_of(p, groups)[k]
            if k == 0:
                for copy in lon_copies[p]:
                    copy.wait_recv()
                merge_halo(p)
            for copy in lat_copies[p, k]:
                copy.wait_recv()
            if k == 0:
                along_lat(p, 0)

            def cells_body(g, carry):
                along_lon(p, g - 1)
                along_lat(p, g)
                return carry

            lax.fori_loop(max(first, 1), first + size, cells_body, 0)
            done = first + size
            if done == groups:
                along_lon(p, groups - 1)
            else:
                done = done - 1
            if p == 2:
                for f in PAIRS[p]:
                    write(f, max(first - 1, 0), done - max(first - 1, 0))

    lane = iota((levels, COLS), 1)
    interpolate(0, range(len(chunks_of(0, groups))))
    write(0, 0, groups)
    write(1, 0, groups)

    def pack_edges(h, carry):
        to_right, to_left = carry
        for n in range(4):
            i = 4 * h + n
            turned = pltpu.roll(u[pl.ds(i * u_step, levels), :], i + 1, 1)
            to_right = jnp.where(lane == i, turned, to_right)
            to_left = jnp.where(lane == i + 1, turned, to_left)
        return to_right, to_left

    nothing = jnp.zeros((levels, COLS), F32)
    to_right, to_left = lax.fori_loop(0, ROWS // 4, pack_edges, (nothing, nothing))
    edge_right[...] = to_right
    edge_left[...] = pltpu.roll(to_left, ROWS - 1, 1)
    v_first[...] = v[u_step : u_step + levels]
    v_last[...] = v[ROWS * u_step : ROWS * u_step + levels]
    edges = [
        send(edge_right, u_west, (a, right)),
        send(edge_left, u_east, (a, left)),
        send(v_last, v_low, (up, s)),
        send(v_first, v_high, (down, s)),
    ]
    count = len(chunks_of(1, groups))
    interpolate(1, range(1))
    for k, (first, size) in enumerate(chunks_of(2, groups)):
        send_rows(2, k, first, size)
    interpolate(1, range(1, count - 1))
    for copy in edges:
        copy.wait_recv()

    v[0:levels] = jnp.where(a == 0, 0.0, v_low[...])
    v[(ROWS + 1) * u_step : (ROWS + 1) * u_step + levels] = jnp.where(
        a == bands - 1, 0.0, v_high[...]
    )
    u_edges[...] = jnp.where(lane < ROWS, u_west[...], u_east[...])

    def diverge(h, carry):
        changes = []
        for m in range(2):
            blocks = []
            for n in range(4):
                i = 8 * h + 4 * m + n
                mine = (lane == i) | (lane == i + ROWS)
                blocks.append(
                    jnp.concatenate(
                        [u[pl.ds(i * u_step, levels), :], jnp.where(mine, u_edges[...], 0.0)], 1
                    )
                )
            changes.append(
                jnp.dot(
                    jnp.concatenate(blocks, 0).astype(BF16), slope[...], preferred_element_type=F32
                )
            )
        for m in range(2):
            for n in range(4):
                i = 8 * h + 4 * m + n
                south = v[pl.ds(i * u_step, levels), :]
                north = v[pl.ds((i + 2) * u_step, levels), :]
                rhs[pl.ds(i * rhs_step + 2 * levels, levels), :] = (
                    changes[m][n * levels : (n + 1) * levels] + 0.5 * (north - south)
                )
        return carry

    lax.fori_loop(0, ROWS // 8, diverge, 0)
    interpolate(1, range(count - 1, count))

    def solve(h, carry):
        for m in range(4):
            i = 8 * h + 2 * m
            both = jnp.concatenate(
                [
                    rhs[pl.ds(i * rhs_step, 3 * levels), :],
                    rhs[pl.ds((i + 1) * rhs_step, 3 * levels), :],
                ],
                1,
            ).astype(BF16)
            answer = jnp.dot(acoustic[...], both, preferred_element_type=F32)
            for c in range(0, 2 * levels, 8):
                at = c * solved_step + i
                solved[pl.ds(at, 8, stride=solved_step), :] = answer[c : c + 8, :COLS]
                solved[pl.ds(at + 1, 8, stride=solved_step), :] = answer[c : c + 8, COLS:]
        return carry

    lax.fori_loop(0, ROWS // 8, solve, 0)

    def round_off(g, carry):
        for q in range(GROUP):
            l = g * GROUP + q
            out[2, l] = solved[pl.ds(l * solved_step, ROWS), :].astype(BF16)
            out[5, l] = solved[pl.ds((l + levels) * solved_step, ROWS), :].astype(BF16)
        return carry

    lax.fori_loop(0, groups, round_off, 0)
    write(2, 0, groups)
    write(5, 0, groups)

    interpolate(2, range(len(chunks_of(2, groups))))
    for copy in sent:
        copy.wait_send()
    for copy in writes:
        copy.wait()


def hand_over(src, dst, held, in_sem, out_sem):
    size = src.shape[1] // PIECES
    pieces = [(f, pl.ds(n * size, size)) for f in range(6) for n in range(PIECES)]
    reads = [
        pltpu.make_async_copy(src.at[f, span], held.at[f, span], in_sem.at[k])
        for k, (f, span) in enumerate(pieces)
    ]
    writes = [
        pltpu.make_async_copy(held.at[f, span], dst.at[f, span], out_sem.at[k])
        for k, (f, span) in enumerate(pieces)
    ]
    for copy in reads:
        copy.start()
    for read, copy in zip(reads, writes):
        read.wait()
        copy.start()
    for copy in writes:
        copy.wait()


def local(bands, sectors, fields, frac_lat, off_lat, frac_lon, off_lon, sound_coef, inverse):
    levels = fields.shape[1]
    groups = levels // GROUP
    doubles = (groups + 1) // 2
    outside = pl.BlockSpec(memory_space=pltpu.HBM)
    halo_rows = pltpu.VMEM((3, levels, 16, COLS), BF16)
    halo_columns = pltpu.VMEM((3, doubles, 2 * ROWS, COLS), BF16)
    corners = pltpu.VMEM((4, 3, doubles, 16, COLS), BF16)
    level_rows = pltpu.VMEM((levels, COLS), F32)
    messages = 2 * sum(len(chunks_of(p, groups)) for p in range(3)) + 18 + 4
    outgoing = 4 + 2 * len(chunks_of(2, groups))
    stepped = pl.pallas_call(
        functools.partial(kernel, levels, bands, sectors),
        out_shape=jax.ShapeDtypeStruct(fields.shape, BF16),
        in_specs=[outside] * 7,
        out_specs=outside,
        scratch_shapes=[
            pltpu.VMEM(fields.shape, BF16),
            pltpu.VMEM(fields.shape, BF16),
            pltpu.VMEM((ROWS, levels), F32),
            pltpu.VMEM((ROWS, levels), jnp.int32),
            pltpu.VMEM((levels, COLS), F32),
            pltpu.VMEM((levels, COLS), jnp.int32),
            pltpu.VMEM((1, levels), F32),
            pltpu.VMEM((2 * levels, 2 * levels), F32),
            pltpu.VMEM((levels, ROWS), F32),
            pltpu.VMEM((levels, ROWS), jnp.int32),
            halo_rows, halo_rows, halo_rows, halo_rows,
            pltpu.VMEM((8, 2 * COLS, 2 * COLS), BF16),
            pltpu.VMEM((3, doubles, 2 * ROWS, 2 * COLS), F32),
            halo_columns, halo_columns, halo_columns, halo_columns,
            corners, corners,
            pltpu.VMEM((3, 2 * doubles, 2, ROWS + 2 * HALO, COLS), BF16),
            pltpu.VMEM((4, levels // 4, COLS), F32),
            pltpu.VMEM((levels // 4, COLS), jnp.int32),
            pltpu.VMEM((levels, ROWS, ROWS + 2 * HALO), BF16),
            pltpu.VMEM((4, levels, COLS), F32),
            level_rows,
            pltpu.VMEM((levels, 2 * COLS, COLS), BF16),
            pltpu.VMEM((GROUP, 2 * ROWS, 2 * COLS), BF16),
            pltpu.VMEM((ROWS * (levels + 1), COLS), F32),
            pltpu.VMEM(((ROWS + 2) * (levels + 1), COLS), F32),
        ]
        + [level_rows] * 9
        + [
            pltpu.VMEM((ROWS * (3 * levels + 1), COLS), F32),
            pltpu.VMEM((2 * levels * (ROWS + 1), COLS), F32),
            pltpu.VMEM((2 * levels, 3 * levels), BF16),
            pltpu.VMEM((2 * COLS, COLS), BF16),
            pltpu.SemaphoreType.DMA((4 + 2 * len(chunks_of(0, groups)) + 6,)),
            pltpu.SemaphoreType.DMA((outgoing,)),
            pltpu.SemaphoreType.DMA((messages,)),
            pltpu.SemaphoreType.DMA((messages,)),
        ],
        compiler_params=pltpu.CompilerParams(
            collective_id=0, has_side_effects=True, vmem_limit_bytes=60 * 2**20
        ),
        cost_estimate=pl.CostEstimate(
            flops=10**9, bytes_accessed=2 * 2 * fields.size, transcendentals=0
        ),
    )(
        fields, frac_lat[:, 0, :].T, off_lat[:, 0, :].T, frac_lon, off_lon,
        sound_coef[None, :], inverse,
    )
    return pl.pallas_call(
        hand_over,
        out_shape=jax.ShapeDtypeStruct(fields.shape, BF16),
        in_specs=[outside],
        out_specs=outside,
        scratch_shapes=[
            pltpu.VMEM(fields.shape, BF16),
            pltpu.SemaphoreType.DMA((6 * PIECES,)),
            pltpu.SemaphoreType.DMA((6 * PIECES,)),
        ],
        compiler_params=pltpu.CompilerParams(vmem_limit_bytes=60 * 2**20),
    )(stepped)


def solution(mesh):
    placed = (
        P(None, None, "lat", "lon"),
        P(None, "lon", "lat"),
        P(None, "lon", "lat"),
        P(None, "lat", "lon"),
        P(None, "lat", "lon"),
        P(),
        P(),
    )
    return jax.shard_map(
        functools.partial(local, mesh.shape["lat"], mesh.shape["lon"]),
        mesh=mesh, in_specs=placed, out_specs=P(None, None, "lat", "lon"), check_vma=False,
    )
```

```python
import functools

import jax
import jax.numpy as jnp
from jax import lax
from jax.experimental import pallas as pl
from jax.experimental.pallas import tpu as pltpu
from jax.sharding import PartitionSpec as P

MESH = pl.DeviceIdType.MESH
HALO = 8
ROWS = 32
COLS = 128
GROUP = 8
FAR = -100000
PAIRS = ((0, 1), (2, 5), (3, 4))
F32 = jnp.float32
BF16 = jnp.bfloat16
LON = BF16
PIECES = 1


def cubic_weights(fraction):
    return (
        -fraction * (fraction - 1.0) * (fraction - 2.0) / 6.0,
        (fraction + 1.0) * (fraction - 1.0) * (fraction - 2.0) / 2.0,
        -(fraction + 1.0) * fraction * (fraction - 2.0) / 2.0,
        (fraction + 1.0) * fraction * (fraction - 1.0) / 6.0,
    )


def chunks_of(pair, groups):
    cuts, first = [], 0
    while first < groups:
        size = min(3, groups - first)
        if pair == len(PAIRS) - 1 and groups - first <= 3:
            size = 1
        cuts.append((first, size))
        first += size
    return cuts


def iota(shape, dim):
    return lax.broadcasted_iota(jnp.int32, shape, dim)


def taps(distance, weights):
    out = jnp.where(distance == 3, weights[3], jnp.zeros((), weights[3].dtype))
    for node in (2, 1, 0):
        out = jnp.where(distance == node, weights[node], out)
    return out


def kernel(
    levels, bands, sectors,
    fields, frac_lat, off_lat, frac_lon, off_lon, sound, inverse, final,
    out, x, frac_lat_in, off_lat_in, frac_lon_in, off_lon_in, sound_in, inverse_in,
    frac_lat_t, off_lat_t,
    send_up, send_down, low, high, picker, packed, send_right, send_left, from_left, from_right,
    send_corner, corner, merged, lat_w, lat_anchor, lat_matrix, lon_w, lon_anchor, lon_matrix,
    interim, u, v, v_first, v_last, v_low, v_high, edge_right, edge_left, u_west, u_east, u_edges,
    rhs, solved, acoustic, slope,
    in_sem, out_sem, send_sem, recv_sem,
):
    groups = levels // GROUP
    doubles = (groups + 1) // 2
    u_step, rhs_step, solved_step = levels + 1, 3 * levels + 1, ROWS + 1
    a = lax.axis_index("lat")
    s = lax.axis_index("lon")
    up, down = lax.rem(a + 1, bands), lax.rem(a + bands - 1, bands)
    right, left = lax.rem(s + 1, sectors), lax.rem(s + sectors - 1, sectors)

    started = []

    def load(src, dst):
        copy = pltpu.make_async_copy(src, dst, in_sem.at[len(started)])
        copy.start()
        started.append(copy)
        return copy

    loads = {}
    for p, pair in enumerate(PAIRS):
        for k, (first, size) in enumerate(chunks_of(p, groups) if p == 0 else [(0, groups)]):
            span = pl.ds(first * GROUP, size * GROUP)
            loads[p, k] = [load(fields.at[f, span], x.at[f, span]) for f in pair]
    small = [
        load(src, dst)
        for src, dst in (
            (frac_lon.at[:, 0, :], frac_lon_in), (off_lon.at[:, 0, :], off_lon_in),
            (frac_lat, frac_lat_in), (off_lat, off_lat_in),
            (sound, sound_in), (inverse, inverse_in),
        )
    ]

    barrier = pltpu.get_barrier_semaphore()
    for there in (
        (down, s), (up, s), (a, left), (a, right),
        (down, left), (down, right), (up, left), (up, right),
    ):
        pl.semaphore_signal(barrier, inc=1, device_id=there, device_id_type=MESH)

    sent = []

    def send(src, dst, there):
        k = len(sent)
        copy = pltpu.make_async_remote_copy(
            src_ref=src, dst_ref=dst, send_sem=send_sem.at[k], recv_sem=recv_sem.at[k],
            device_id=there, device_id_type=MESH,
        )
        copy.start()
        sent.append(copy)
        return copy

    def pack_rows(p, first, size):
        fa, fb = PAIRS[p]

        def rows_body(g, carry):
            for q in range(GROUP):
                l = g * GROUP + q
                xa, xb = x[fa, l].astype(F32), x[fb, l].astype(F32)
                send_up[p, l] = jnp.concatenate([xa[24:32], xb[24:32]], 0).astype(BF16)
                send_down[p, l] = jnp.concatenate([xa[0:8], xb[0:8]], 0).astype(BF16)
            return carry

        lax.fori_loop(first, first + size, rows_body, 0)

    def build_picker(t, carry):
        k = iota((2 * COLS, COLS), 0)
        column = k & (COLS - 1)
        q = 2 * t + jnp.where(k >= COLS, 1, 0)
        slot = 16 * (q & 7)
        second = q & 8
        target = jnp.where(
            column >= COLS - HALO,
            slot + second + column - (COLS - HALO),
            jnp.where(column < HALO, COLS + slot + (8 - second) + column, -1),
        )
        lane = iota((2 * COLS, COLS), 1)
        picker[t, :, 0:COLS] = jnp.where(target == lane, 1.0, 0.0).astype(BF16)
        picker[t, :, COLS:] = jnp.where(target == lane + COLS, 1.0, 0.0).astype(BF16)
        return carry

    lax.fori_loop(0, 8, build_picker, 0)

    def pack_columns(pairs):
        for t in range(8):
            rows = []
            for p in pairs:
                for d in range(doubles):
                    l = 16 * d + 2 * t
                    if l < levels:
                        for f in PAIRS[p]:
                            rows.append(jnp.concatenate([x[f, l], x[f, l + 1]], 1))
            part = jnp.dot(jnp.concatenate(rows, 0), picker[t], preferred_element_type=F32)
            at = 0
            for p in pairs:
                for d in range(doubles):
                    if 16 * d + 2 * t < levels:
                        block = part[at : at + 2 * ROWS]
                        at += 2 * ROWS
                        packed[p, d] = block if t == 0 else packed[p, d] + block
        for p in pairs:

            def merge(d, carry):
                block = packed[p, d]
                to_right, to_left = block[:, :COLS], block[:, COLS:]
                send_right[p, d] = to_right.astype(BF16)
                send_left[p, d] = to_left.astype(BF16)
                for c, (side, row) in enumerate(
                    ((to_left, 0), (to_right, 0), (to_left, 24), (to_right, 24))
                ):
                    send_corner[c, p, d] = jnp.concatenate(
                        [side[row : row + 8], side[row + 32 : row + 40]], 0
                    ).astype(BF16)
                return carry

            lax.fori_loop(0, doubles, merge, 0)

    lat_copies, lon_copies = {}, {}

    def send_rows(p, k, first, size):
        span = pl.ds(first * GROUP, size * GROUP)
        lat_copies[p, k] = (
            send(send_up.at[p, span], low.at[p, span], (up, s)),
            send(send_down.at[p, span], high.at[p, span], (down, s)),
        )

    def send_columns(p):
        lon_copies[p] = [
            send(send_corner.at[c, p], corner.at[c, p], there)
            for c, there in enumerate(((down, left), (down, right), (up, left), (up, right)))
        ]
        lon_copies[p].append(send(send_right.at[p], from_left.at[p], (a, right)))
        lon_copies[p].append(send(send_left.at[p], from_right.at[p], (a, left)))

    for k, (first, size) in enumerate(chunks_of(0, groups)):
        for copy in loads[0, k]:
            copy.wait()
        pack_rows(0, first, size)
        if k == 0:
            pl.semaphore_wait(barrier, 8)
            send_rows(0, k, first, size)
    pack_columns([0])
    send_columns(0)
    send_rows(0, 1, *chunks_of(0, groups)[1])
    for p in (1, 2):
        for copy in loads[p, 0]:
            copy.wait()
        pack_rows(p, 0, groups)
    pack_columns([1, 2])
    send_rows(0, 2, *chunks_of(0, groups)[2])
    for k, (first, size) in enumerate(chunks_of(1, groups)):
        send_rows(1, k, first, size)
    send_columns(1)
    send_columns(2)
    for copy in small:
        copy.wait()

    rounded = [w.astype(BF16).astype(F32) for w in cubic_weights(frac_lon_in[...])]
    for node in range(4):
        lon_w[node] = rounded[node]
    lon_anchor[...] = (off_lon_in[...] + iota(lon_anchor.shape, 1) + (HALO - 1)).astype(F32)

    place = (iota((COLS, COLS), 0) + HALO).astype(F32).astype(LON)
    r16 = iota((16, COLS), 0)
    left_first = jnp.where(r16 < 8, r16, r16 - 8 + HALO + COLS).astype(F32)
    right_first = jnp.where(r16 < 8, r16 + HALO + COLS, r16 - 8).astype(F32)

    def build_lon(g, carry):
        edge_place = jnp.where((g & 1) == 0, left_first, right_first).astype(LON)
        for q in range(GROUP):
            l = g * GROUP + q
            anchor = jnp.broadcast_to(lon_anchor[pl.ds(l, 1), :], (16, COLS)).astype(LON)
            weights = [
                jnp.broadcast_to(lon_w[node, pl.ds(l, 1), :], (16, COLS)).astype(LON)
                for node in range(4)
            ]
            for t in range(0, COLS, 16):
                lon_matrix[l, t : t + 16] = taps(place[t : t + 16] - anchor, weights).astype(BF16)
            lon_matrix[l, COLS:] = jnp.zeros((COLS, COLS), BF16)
            lon_matrix[l, COLS + 16 * q : COLS + 16 * q + 16] = taps(
                edge_place - anchor, weights
            ).astype(BF16)
        return carry

    lax.fori_loop(0, groups, build_lon, 0)

    frac_lat_t[...] = frac_lat_in[...].T
    off_lat_t[...] = off_lat_in[...].T
    quarter = levels // 4
    lane_row = iota((quarter, COLS), 1)

    def side_by_side(ref):
        total = None
        for q in range(4):
            part = ref[pl.ds(q, quarter, stride=4), :]
            part = jnp.concatenate([part] * 4, 1)
            total = part if total is None else jnp.where(lane_row >= ROWS * q, part, total)
        return total

    rounded = [w.astype(BF16).astype(F32) for w in cubic_weights(side_by_side(frac_lat_t))]
    for node in range(4):
        lat_w[node] = rounded[node]
    lat_anchor[...] = side_by_side(off_lat_t) + (lane_row & (ROWS - 1)) + (HALO - 1)

    r = iota((ROWS + 2 * HALO, COLS), 0)
    below = jnp.where(a == 0, FAR, r - ROWS)
    above = jnp.where(a == bands - 1, FAR, r)
    row_place = jnp.where(r < ROWS, r + HALO, jnp.where(r < ROWS + HALO, below, above))

    def build_lat(h, carry):
        turned = []
        for n in range(3):
            j = 3 * h + n
            distance = row_place - lat_anchor[pl.ds(j, 1), :]
            weights = [lat_w[node, pl.ds(j, 1), :] for node in range(4)]
            turned.append(taps(distance, weights).astype(BF16).T)
        for n in range(3):
            for q in range(4):
                lat_matrix[4 * (3 * h + n) + q] = turned[n][ROWS * q : ROWS * q + ROWS]
        return carry

    lax.fori_loop(0, quarter // 3, build_lat, 0)

    inv = inverse_in[...]
    acoustic[...] = jnp.concatenate([inv, -(inv[:, levels:] * sound_in[...])], 1).astype(BF16)
    k, j = iota(slope.shape, 0), iota(slope.shape, 1)
    minus = ((k < COLS) & (k == j - 1)) | ((k >= COLS) & (k < COLS + ROWS) & (j == 0))
    plus = ((k < COLS) & (k == j + 1)) | (
        (k >= COLS + ROWS) & (k < COLS + 2 * ROWS) & (j == COLS - 1)
    )
    slope[...] = jnp.where(plus, 0.5, jnp.where(minus, -0.5, 0.0)).astype(BF16)

    even64 = (iota((2 * ROWS, COLS), 1) & 8) == 0
    even16 = (iota((16, COLS), 1) & 8) == 0

    def merge_halo(p):
        def halo_body(d, carry):
            l_in, r_in = from_left[p, d].astype(F32), from_right[p, d].astype(F32)
            mine = jnp.where(even64, l_in, r_in), jnp.where(even64, r_in, l_in)
            low_l, low_r = corner[3, p, d].astype(F32), corner[2, p, d].astype(F32)
            high_l, high_r = corner[1, p, d].astype(F32), corner[0, p, d].astype(F32)
            lows = jnp.where(even16, low_l, low_r), jnp.where(even16, low_r, low_l)
            highs = jnp.where(even16, high_l, high_r), jnp.where(even16, high_r, high_l)
            for n in range(2):
                for f in range(2):
                    merged[p, 2 * d + n, f] = jnp.concatenate(
                        [
                            mine[n][ROWS * f : ROWS * f + ROWS],
                            lows[n][8 * f : 8 * f + 8],
                            highs[n][8 * f : 8 * f + 8],
                        ],
                        0,
                    ).astype(BF16)
            return carry

        lax.fori_loop(0, doubles, halo_body, 0)

    def along_lat(p, g):
        fa, fb = PAIRS[p]
        for q in range(GROUP):
            l = g * GROUP + q
            below, above = low[p, l].astype(F32), high[p, l].astype(F32)
            around = [
                jnp.concatenate([below[n : n + 8], above[n : n + 8]], 0).astype(BF16)
                for n in (0, 8)
            ]
            block = jnp.concatenate(
                [
                    jnp.concatenate([x[fa, l], around[0]], 0),
                    merged[p, g, 0],
                    jnp.concatenate([x[fb, l], around[1]], 0),
                    merged[p, g, 1],
                ],
                1,
            )
            y = jnp.dot(lat_matrix[l], block, preferred_element_type=F32).astype(BF16)
            interim[q] = jnp.concatenate([y[:, : 2 * COLS], y[:, 2 * COLS :]], 0)

    def along_lon(p, g):
        fa, fb = PAIRS[p]
        for q in range(GROUP):
            l = g * GROUP + q
            z = jnp.dot(interim[q], lon_matrix[l], preferred_element_type=F32).astype(BF16)
            one, two = z[:ROWS], z[ROWS:]
            if p != 1:
                out[fa, l] = one
                out[fb, l] = two
            if p < 2:
                one, two = one.astype(F32), two.astype(F32)
                for i in range(0, ROWS, 8):
                    if p == 0:
                        u[pl.ds(i * u_step + l, 8, stride=u_step), :] = one[i : i + 8]
                        v[pl.ds((i + 1) * u_step + l, 8, stride=u_step), :] = two[i : i + 8]
                    else:
                        at = i * rhs_step + l
                        rhs[pl.ds(at, 8, stride=rhs_step), :] = one[i : i + 8]
                        rhs[pl.ds(at + levels, 8, stride=rhs_step), :] = two[i : i + 8]

    writes = []

    def write(f, first, size):
        span = pl.ds(first * GROUP, size * GROUP)
        copy = pltpu.make_async_copy(out.at[f, span], final.at[f, span], out_sem.at[len(writes)])
        copy.start()
        writes.append(copy)

    def interpolate(p, chunks):
        for k in chunks:
            first, size = chunks_of(p, groups)[k]
            if k == 0:
                for copy in lon_copies[p]:
                    copy.wait_recv()
                merge_halo(p)
            for copy in lat_copies[p, k]:
                copy.wait_recv()
            if k == 0:
                along_lat(p, 0)

            def cells_body(g, carry):
                along_lon(p, g - 1)
                along_lat(p, g)
                return carry

            lax.fori_loop(max(first, 1), first + size, cells_body, 0)
            done = first + size
            if done == groups:
                along_lon(p, groups - 1)
            else:
                done = done - 1
            if p == 2:
                for f in PAIRS[p]:
                    write(f, max(first - 1, 0), done - max(first - 1, 0))

    lane = iota((levels, COLS), 1)
    for k, (first, size) in enumerate(chunks_of(2, groups)):
        send_rows(2, k, first, size)
    interpolate(0, range(len(chunks_of(0, groups))))
    write(0, 0, groups)
    write(1, 0, groups)

    def pack_edges(h, carry):
        to_right, to_left = carry
        for n in range(8):
            i = 8 * h + n
            turned = pltpu.roll(u[pl.ds(i * u_step, levels), :], i + 1, 1)
            to_right = jnp.where(lane == i, turned, to_right)
            to_left = jnp.where(lane == i + 1, turned, to_left)
        return to_right, to_left

    nothing = jnp.zeros((levels, COLS), F32)
    to_right, to_left = lax.fori_loop(0, ROWS // 8, pack_edges, (nothing, nothing))
    edge_right[...] = to_right
    edge_left[...] = pltpu.roll(to_left, ROWS - 1, 1)
    v_first[...] = v[u_step : u_step + levels]
    v_last[...] = v[ROWS * u_step : ROWS * u_step + levels]
    edges = [
        send(edge_right, u_west, (a, right)),
        send(edge_left, u_east, (a, left)),
        send(v_last, v_low, (up, s)),
        send(v_first, v_high, (down, s)),
    ]
    count = len(chunks_of(1, groups))
    interpolate(1, range(count - 1))
    interpolate(1, range(count - 1, count))
    interpolate(2, range(4))
    for copy in edges:
        copy.wait_recv()

    v[0:levels] = jnp.where(a == 0, 0.0, v_low[...])
    v[(ROWS + 1) * u_step : (ROWS + 1) * u_step + levels] = jnp.where(
        a == bands - 1, 0.0, v_high[...]
    )
    u_edges[...] = jnp.where(lane < ROWS, u_west[...], u_east[...])

    def diverge(h, carry):
        changes = []
        for m in range(2):
            blocks = []
            for n in range(4):
                i = 8 * h + 4 * m + n
                mine = (lane == i) | (lane == i + ROWS)
                blocks.append(
                    jnp.concatenate(
                        [u[pl.ds(i * u_step, levels), :], jnp.where(mine, u_edges[...], 0.0)], 1
                    )
                )
            changes.append(
                jnp.dot(
                    jnp.concatenate(blocks, 0).astype(BF16), slope[...], preferred_element_type=F32
                )
            )
        for m in range(2):
            for n in range(4):
                i = 8 * h + 4 * m + n
                south = v[pl.ds(i * u_step, levels), :]
                north = v[pl.ds((i + 2) * u_step, levels), :]
                rhs[pl.ds(i * rhs_step + 2 * levels, levels), :] = (
                    changes[m][n * levels : (n + 1) * levels] + 0.5 * (north - south)
                )
        return carry

    lax.fori_loop(0, ROWS // 8, diverge, 0)

    def solve(h, carry):
        for m in range(4):
            i = 8 * h + 2 * m
            both = jnp.concatenate(
                [
                    rhs[pl.ds(i * rhs_step, 3 * levels), :],
                    rhs[pl.ds((i + 1) * rhs_step, 3 * levels), :],
                ],
                1,
            ).astype(BF16)
            answer = jnp.dot(acoustic[...], both, preferred_element_type=F32)
            for c in range(0, 2 * levels, 8):
                at = c * solved_step + i
                solved[pl.ds(at, 8, stride=solved_step), :] = answer[c : c + 8, :COLS]
                solved[pl.ds(at + 1, 8, stride=solved_step), :] = answer[c : c + 8, COLS:]
        return carry

    lax.fori_loop(0, ROWS // 8, solve, 0)

    def round_off(g, carry):
        for q in range(GROUP):
            l = g * GROUP + q
            out[2, l] = solved[pl.ds(l * solved_step, ROWS), :].astype(BF16)
            out[5, l] = solved[pl.ds((l + levels) * solved_step, ROWS), :].astype(BF16)
        return carry

    lax.fori_loop(0, groups, round_off, 0)
    write(2, 0, groups)
    write(5, 0, groups)

    interpolate(2, range(4, len(chunks_of(2, groups))))
    for copy in sent:
        copy.wait_send()
    for copy in writes:
        copy.wait()


def hand_over(src, dst, held, in_sem, out_sem):
    size = src.shape[1] // PIECES
    pieces = [(f, pl.ds(n * size, size)) for f in range(6) for n in range(PIECES)]
    reads = [
        pltpu.make_async_copy(src.at[f, span], held.at[f, span], in_sem.at[k])
        for k, (f, span) in enumerate(pieces)
    ]
    writes = [
        pltpu.make_async_copy(held.at[f, span], dst.at[f, span], out_sem.at[k])
        for k, (f, span) in enumerate(pieces)
    ]
    for copy in reads:
        copy.start()
    for read, copy in zip(reads, writes):
        read.wait()
        copy.start()
    for copy in writes:
        copy.wait()


def local(bands, sectors, fields, frac_lat, off_lat, frac_lon, off_lon, sound_coef, inverse):
    levels = fields.shape[1]
    groups = levels // GROUP
    doubles = (groups + 1) // 2
    outside = pl.BlockSpec(memory_space=pltpu.HBM)
    halo_rows = pltpu.VMEM((3, levels, 16, COLS), BF16)
    halo_columns = pltpu.VMEM((3, doubles, 2 * ROWS, COLS), BF16)
    corners = pltpu.VMEM((4, 3, doubles, 16, COLS), BF16)
    level_rows = pltpu.VMEM((levels, COLS), F32)
    messages = 2 * sum(len(chunks_of(p, groups)) for p in range(3)) + 18 + 4
    outgoing = 4 + 2 * len(chunks_of(2, groups))
    stepped = pl.pallas_call(
        functools.partial(kernel, levels, bands, sectors),
        out_shape=jax.ShapeDtypeStruct(fields.shape, BF16),
        in_specs=[outside] * 7,
        out_specs=outside,
        scratch_shapes=[
            pltpu.VMEM(fields.shape, BF16),
            pltpu.VMEM(fields.shape, BF16),
            pltpu.VMEM((ROWS, levels), F32),
            pltpu.VMEM((ROWS, levels), jnp.int32),
            pltpu.VMEM((levels, COLS), F32),
            pltpu.VMEM((levels, COLS), jnp.int32),
            pltpu.VMEM((1, levels), F32),
            pltpu.VMEM((2 * levels, 2 * levels), F32),
            pltpu.VMEM((levels, ROWS), F32),
            pltpu.VMEM((levels, ROWS), jnp.int32),
            halo_rows, halo_rows, halo_rows, halo_rows,
            pltpu.VMEM((8, 2 * COLS, 2 * COLS), BF16),
            pltpu.VMEM((3, doubles, 2 * ROWS, 2 * COLS), F32),
            halo_columns, halo_columns, halo_columns, halo_columns,
            corners, corners,
            pltpu.VMEM((3, 2 * doubles, 2, ROWS + 2 * HALO, COLS), BF16),
            pltpu.VMEM((4, levels // 4, COLS), F32),
            pltpu.VMEM((levels // 4, COLS), jnp.int32),
            pltpu.VMEM((levels, ROWS, ROWS + 2 * HALO), BF16),
            pltpu.VMEM((4, levels, COLS), F32),
            level_rows,
            pltpu.VMEM((levels, 2 * COLS, COLS), BF16),
            pltpu.VMEM((GROUP, 2 * ROWS, 2 * COLS), BF16),
            pltpu.VMEM((ROWS * (levels + 1), COLS), F32),
            pltpu.VMEM(((ROWS + 2) * (levels + 1), COLS), F32),
        ]
        + [level_rows] * 9
        + [
            pltpu.VMEM((ROWS * (3 * levels + 1), COLS), F32),
            pltpu.VMEM((2 * levels * (ROWS + 1), COLS), F32),
            pltpu.VMEM((2 * levels, 3 * levels), BF16),
            pltpu.VMEM((2 * COLS, COLS), BF16),
            pltpu.SemaphoreType.DMA((4 + 2 * len(chunks_of(0, groups)) + 6,)),
            pltpu.SemaphoreType.DMA((outgoing,)),
            pltpu.SemaphoreType.DMA((messages,)),
            pltpu.SemaphoreType.DMA((messages,)),
        ],
        compiler_params=pltpu.CompilerParams(
            collective_id=0, has_side_effects=True, vmem_limit_bytes=60 * 2**20
        ),
        cost_estimate=pl.CostEstimate(
            flops=10**9, bytes_accessed=2 * 2 * fields.size, transcendentals=0
        ),
    )(
        fields, frac_lat[:, 0, :].T, off_lat[:, 0, :].T, frac_lon, off_lon,
        sound_coef[None, :], inverse,
    )
    return pl.pallas_call(
        hand_over,
        out_shape=jax.ShapeDtypeStruct(fields.shape, BF16),
        in_specs=[outside],
        out_specs=outside,
        scratch_shapes=[
            pltpu.VMEM(fields.shape, BF16),
            pltpu.SemaphoreType.DMA((6 * PIECES,)),
            pltpu.SemaphoreType.DMA((6 * PIECES,)),
        ],
        compiler_params=pltpu.CompilerParams(vmem_limit_bytes=60 * 2**20),
    )(stepped)


def solution(mesh):
    placed = (
        P(None, None, "lat", "lon"),
        P(None, "lon", "lat"),
        P(None, "lon", "lat"),
        P(None, "lat", "lon"),
        P(None, "lat", "lon"),
        P(),
        P(),
    )
    return jax.shard_map(
        functools.partial(local, mesh.shape["lat"], mesh.shape["lon"]),
        mesh=mesh, in_specs=placed, out_specs=P(None, None, "lat", "lon"), check_vma=False,
    )
```

```python
import functools

import jax
import jax.numpy as jnp
from jax import lax
from jax.experimental import pallas as pl
from jax.experimental.pallas import tpu as pltpu
from jax.sharding import PartitionSpec as P

MESH = pl.DeviceIdType.MESH
HALO = 8
ROWS = 32
COLS = 128
GROUP = 8
FAR = -100000
PAIRS = ((0, 1), (2, 5), (3, 4))
F32 = jnp.float32
BF16 = jnp.bfloat16
LON = BF16
PIECES = 1


def cubic_weights(fraction):
    return (
        -fraction * (fraction - 1.0) * (fraction - 2.0) / 6.0,
        (fraction + 1.0) * (fraction - 1.0) * (fraction - 2.0) / 2.0,
        -(fraction + 1.0) * fraction * (fraction - 2.0) / 2.0,
        (fraction + 1.0) * fraction * (fraction - 1.0) / 6.0,
    )


def chunks_of(pair, groups):
    cuts, first = [], 0
    while first < groups:
        size = min(3, groups - first)
        if pair == len(PAIRS) - 1 and groups - first <= 3:
            size = 1
        cuts.append((first, size))
        first += size
    return cuts


def iota(shape, dim):
    return lax.broadcasted_iota(jnp.int32, shape, dim)


def taps(distance, weights):
    out = jnp.where(distance == 3, weights[3], jnp.zeros((), weights[3].dtype))
    for node in (2, 1, 0):
        out = jnp.where(distance == node, weights[node], out)
    return out


def kernel(
    levels, bands, sectors,
    fields, frac_lat, off_lat, frac_lon, off_lon, sound, inverse, final,
    out, x, frac_lat_in, off_lat_in, frac_lon_in, off_lon_in, sound_in, inverse_in,
    frac_lat_t, off_lat_t,
    send_up, send_down, low, high, picker, packed, send_right, send_left, from_left, from_right,
    send_corner, corner, merged, lat_w, lat_anchor, lat_matrix, lon_w, lon_anchor, lon_matrix,
    interim, u, v, v_first, v_last, v_low, v_high, edge_right, edge_left, u_west, u_east, u_edges,
    rhs, solved, acoustic, slope,
    in_sem, out_sem, send_sem, recv_sem,
):
    groups = levels // GROUP
    doubles = (groups + 1) // 2
    u_step, rhs_step, solved_step = levels + 1, 3 * levels + 1, ROWS + 1
    a = lax.axis_index("lat")
    s = lax.axis_index("lon")
    up, down = lax.rem(a + 1, bands), lax.rem(a + bands - 1, bands)
    right, left = lax.rem(s + 1, sectors), lax.rem(s + sectors - 1, sectors)

    started = []

    def load(src, dst):
        copy = pltpu.make_async_copy(src, dst, in_sem.at[len(started)])
        copy.start()
        started.append(copy)
        return copy

    loads = {}
    for p, pair in enumerate(PAIRS):
        for k, (first, size) in enumerate(chunks_of(p, groups) if p == 0 else [(0, groups)]):
            span = pl.ds(first * GROUP, size * GROUP)
            loads[p, k] = [load(fields.at[f, span], x.at[f, span]) for f in pair]
    small = [
        load(src, dst)
        for src, dst in (
            (frac_lon.at[:, 0, :], frac_lon_in), (off_lon.at[:, 0, :], off_lon_in),
            (frac_lat, frac_lat_in), (off_lat, off_lat_in),
            (sound, sound_in), (inverse, inverse_in),
        )
    ]

    barrier = pltpu.get_barrier_semaphore()
    for there in (
        (down, s), (up, s), (a, left), (a, right),
        (down, left), (down, right), (up, left), (up, right),
    ):
        pl.semaphore_signal(barrier, inc=1, device_id=there, device_id_type=MESH)

    sent = []

    def send(src, dst, there):
        k = len(sent)
        copy = pltpu.make_async_remote_copy(
            src_ref=src, dst_ref=dst, send_sem=send_sem.at[k], recv_sem=recv_sem.at[k],
            device_id=there, device_id_type=MESH,
        )
        copy.start()
        sent.append(copy)
        return copy

    def pack_rows(p, first, size):
        fa, fb = PAIRS[p]

        def rows_body(g, carry):
            for q in range(GROUP):
                l = g * GROUP + q
                xa, xb = x[fa, l].astype(F32), x[fb, l].astype(F32)
                send_up[p, l] = jnp.concatenate([xa[24:32], xb[24:32]], 0).astype(BF16)
                send_down[p, l] = jnp.concatenate([xa[0:8], xb[0:8]], 0).astype(BF16)
            return carry

        lax.fori_loop(first, first + size, rows_body, 0)

    def build_picker(t, carry):
        k = iota((2 * COLS, COLS), 0)
        column = k & (COLS - 1)
        q = 2 * t + jnp.where(k >= COLS, 1, 0)
        slot = 16 * (q & 7)
        second = q & 8
        target = jnp.where(
            column >= COLS - HALO,
            slot + second + column - (COLS - HALO),
            jnp.where(column < HALO, COLS + slot + (8 - second) + column, -1),
        )
        lane = iota((2 * COLS, COLS), 1)
        picker[t, :, 0:COLS] = jnp.where(target == lane, 1.0, 0.0).astype(BF16)
        picker[t, :, COLS:] = jnp.where(target == lane + COLS, 1.0, 0.0).astype(BF16)
        return carry

    lax.fori_loop(0, 8, build_picker, 0)

    def pack_columns(pairs):
        for t in range(8):
            rows = []
            for p in pairs:
                for d in range(doubles):
                    l = 16 * d + 2 * t
                    if l < levels:
                        for f in PAIRS[p]:
                            rows.append(jnp.concatenate([x[f, l], x[f, l + 1]], 1))
            part = jnp.dot(jnp.concatenate(rows, 0), picker[t], preferred_element_type=F32)
            at = 0
            for p in pairs:
                for d in range(doubles):
                    if 16 * d + 2 * t < levels:
                        block = part[at : at + 2 * ROWS]
                        at += 2 * ROWS
                        packed[p, d] = block if t == 0 else packed[p, d] + block
        for p in pairs:

            def merge(d, carry):
                block = packed[p, d]
                to_right, to_left = block[:, :COLS], block[:, COLS:]
                send_right[p, d] = to_right.astype(BF16)
                send_left[p, d] = to_left.astype(BF16)
                for c, (side, row) in enumerate(
                    ((to_left, 0), (to_right, 0), (to_left, 24), (to_right, 24))
                ):
                    send_corner[c, p, d] = jnp.concatenate(
                        [side[row : row + 8], side[row + 32 : row + 40]], 0
                    ).astype(BF16)
                return carry

            lax.fori_loop(0, doubles, merge, 0)

    lat_copies, lon_copies = {}, {}

    def send_rows(p, k, first, size):
        span = pl.ds(first * GROUP, size * GROUP)
        lat_copies[p, k] = (
            send(send_up.at[p, span], low.at[p, span], (up, s)),
            send(send_down.at[p, span], high.at[p, span], (down, s)),
        )

    def send_columns(p):
        lon_copies[p] = [
            send(send_corner.at[c, p], corner.at[c, p], there)
            for c, there in enumerate(((down, left), (down, right), (up, left), (up, right)))
        ]
        lon_copies[p].append(send(send_right.at[p], from_left.at[p], (a, right)))
        lon_copies[p].append(send(send_left.at[p], from_right.at[p], (a, left)))

    for k, (first, size) in enumerate(chunks_of(0, groups)):
        for copy in loads[0, k]:
            copy.wait()
        pack_rows(0, first, size)
        if k == 0:
            pl.semaphore_wait(barrier, 8)
            send_rows(0, k, first, size)
    pack_columns([0])
    send_columns(0)
    send_rows(0, 1, *chunks_of(0, groups)[1])
    for p in (1, 2):
        for copy in loads[p, 0]:
            copy.wait()
        pack_rows(p, 0, groups)
    pack_columns([1, 2])
    send_rows(0, 2, *chunks_of(0, groups)[2])
    for k, (first, size) in enumerate(chunks_of(1, groups)):
        send_rows(1, k, first, size)
    send_columns(1)
    send_columns(2)
    for copy in small:
        copy.wait()

    rounded = [w.astype(BF16).astype(F32) for w in cubic_weights(frac_lon_in[...])]
    for node in range(4):
        lon_w[node] = rounded[node]
    lon_anchor[...] = (off_lon_in[...] + iota(lon_anchor.shape, 1) + (HALO - 1)).astype(F32)

    place = (iota((COLS, COLS), 0) + HALO).astype(F32).astype(LON)
    r16 = iota((16, COLS), 0)
    left_first = jnp.where(r16 < 8, r16, r16 - 8 + HALO + COLS).astype(F32)
    right_first = jnp.where(r16 < 8, r16 + HALO + COLS, r16 - 8).astype(F32)

    def build_lon(g, carry):
        edge_place = jnp.where((g & 1) == 0, left_first, right_first).astype(LON)
        for q in range(GROUP):
            l = g * GROUP + q
            anchor = jnp.broadcast_to(lon_anchor[pl.ds(l, 1), :], (16, COLS)).astype(LON)
            weights = [
                jnp.broadcast_to(lon_w[node, pl.ds(l, 1), :], (16, COLS)).astype(LON)
                for node in range(4)
            ]
            for t in range(0, COLS, 16):
                lon_matrix[l, t : t + 16] = taps(place[t : t + 16] - anchor, weights).astype(BF16)
            lon_matrix[l, COLS:] = jnp.zeros((COLS, COLS), BF16)
            lon_matrix[l, COLS + 16 * q : COLS + 16 * q + 16] = taps(
                edge_place - anchor, weights
            ).astype(BF16)
        return carry

    lax.fori_loop(0, groups, build_lon, 0)

    frac_lat_t[...] = frac_lat_in[...].T
    off_lat_t[...] = off_lat_in[...].T
    quarter = levels // 4
    lane_row = iota((quarter, COLS), 1)

    def side_by_side(ref):
        total = None
        for q in range(4):
            part = ref[pl.ds(q, quarter, stride=4), :]
            part = jnp.concatenate([part] * 4, 1)
            total = part if total is None else jnp.where(lane_row >= ROWS * q, part, total)
        return total

    rounded = [w.astype(BF16).astype(F32) for w in cubic_weights(side_by_side(frac_lat_t))]
    for node in range(4):
        lat_w[node] = rounded[node]
    lat_anchor[...] = side_by_side(off_lat_t) + (lane_row & (ROWS - 1)) + (HALO - 1)

    r = iota((ROWS + 2 * HALO, COLS), 0)
    below = jnp.where(a == 0, FAR, r - ROWS)
    above = jnp.where(a == bands - 1, FAR, r)
    row_place = jnp.where(r < ROWS, r + HALO, jnp.where(r < ROWS + HALO, below, above))

    def build_lat(h, carry):
        turned = []
        for n in range(3):
            j = 3 * h + n
            distance = row_place - lat_anchor[pl.ds(j, 1), :]
            weights = [lat_w[node, pl.ds(j, 1), :] for node in range(4)]
            turned.append(taps(distance, weights).astype(BF16).T)
        for n in range(3):
            for q in range(4):
                lat_matrix[4 * (3 * h + n) + q] = turned[n][ROWS * q : ROWS * q + ROWS]
        return carry

    lax.fori_loop(0, quarter // 3, build_lat, 0)

    inv = inverse_in[...]
    acoustic[...] = jnp.concatenate([inv, -(inv[:, levels:] * sound_in[...])], 1).astype(BF16)
    k, j = iota(slope.shape, 0), iota(slope.shape, 1)
    minus = ((k < COLS) & (k == j - 1)) | ((k >= COLS) & (k < COLS + ROWS) & (j == 0))
    plus = ((k < COLS) & (k == j + 1)) | (
        (k >= COLS + ROWS) & (k < COLS + 2 * ROWS) & (j == COLS - 1)
    )
    slope[...] = jnp.where(plus, 0.5, jnp.where(minus, -0.5, 0.0)).astype(BF16)

    even64 = (iota((2 * ROWS, COLS), 1) & 8) == 0
    even16 = (iota((16, COLS), 1) & 8) == 0

    def merge_halo(p):
        def halo_body(d, carry):
            l_in, r_in = from_left[p, d].astype(F32), from_right[p, d].astype(F32)
            mine = jnp.where(even64, l_in, r_in), jnp.where(even64, r_in, l_in)
            low_l, low_r = corner[3, p, d].astype(F32), corner[2, p, d].astype(F32)
            high_l, high_r = corner[1, p, d].astype(F32), corner[0, p, d].astype(F32)
            lows = jnp.where(even16, low_l, low_r), jnp.where(even16, low_r, low_l)
            highs = jnp.where(even16, high_l, high_r), jnp.where(even16, high_r, high_l)
            for n in range(2):
                for f in range(2):
                    merged[p, 2 * d + n, f] = jnp.concatenate(
                        [
                            mine[n][ROWS * f : ROWS * f + ROWS],
                            lows[n][8 * f : 8 * f + 8],
                            highs[n][8 * f : 8 * f + 8],
                        ],
                        0,
                    ).astype(BF16)
            return carry

        lax.fori_loop(0, doubles, halo_body, 0)

    def along_lat(p, g):
        fa, fb = PAIRS[p]
        for q in range(GROUP):
            l = g * GROUP + q
            below, above = low[p, l].astype(F32), high[p, l].astype(F32)
            around = [
                jnp.concatenate([below[n : n + 8], above[n : n + 8]], 0).astype(BF16)
                for n in (0, 8)
            ]
            block = jnp.concatenate(
                [
                    jnp.concatenate([x[fa, l], around[0]], 0),
                    merged[p, g, 0],
                    jnp.concatenate([x[fb, l], around[1]], 0),
                    merged[p, g, 1],
                ],
                1,
            )
            y = jnp.dot(lat_matrix[l], block, preferred_element_type=F32).astype(BF16)
            interim[q] = jnp.concatenate([y[:, : 2 * COLS], y[:, 2 * COLS :]], 0)

    def along_lon(p, g):
        fa, fb = PAIRS[p]
        for q in range(GROUP):
            l = g * GROUP + q
            z = jnp.dot(interim[q], lon_matrix[l], preferred_element_type=F32).astype(BF16)
            one, two = z[:ROWS], z[ROWS:]
            if p != 1:
                out[fa, l] = one
                out[fb, l] = two
            if p < 2:
                one, two = one.astype(F32), two.astype(F32)
                for i in range(0, ROWS, 8):
                    if p == 0:
                        u[pl.ds(i * u_step + l, 8, stride=u_step), :] = one[i : i + 8]
                        v[pl.ds((i + 1) * u_step + l, 8, stride=u_step), :] = two[i : i + 8]
                    else:
                        at = i * rhs_step + l
                        rhs[pl.ds(at, 8, stride=rhs_step), :] = one[i : i + 8]
                        rhs[pl.ds(at + levels, 8, stride=rhs_step), :] = two[i : i + 8]

    writes = []

    def write(f, first, size):
        span = pl.ds(first * GROUP, size * GROUP)
        copy = pltpu.make_async_copy(out.at[f, span], final.at[f, span], out_sem.at[len(writes)])
        copy.start()
        writes.append(copy)

    def interpolate(p, chunks):
        for k in chunks:
            first, size = chunks_of(p, groups)[k]
            if k == 0:
                for copy in lon_copies[p]:
                    copy.wait_recv()
                merge_halo(p)
            for copy in lat_copies[p, k]:
                copy.wait_recv()
            if k == 0:
                along_lat(p, 0)

            def cells_body(g, carry):
                along_lon(p, g - 1)
                along_lat(p, g)
                return carry

            lax.fori_loop(max(first, 1), first + size, cells_body, 0)
            done = first + size
            if done == groups:
                along_lon(p, groups - 1)
            else:
                done = done - 1
            if p == 2:
                for f in PAIRS[p]:
                    write(f, max(first - 1, 0), done - max(first - 1, 0))

    lane = iota((levels, COLS), 1)
    for k, (first, size) in enumerate(chunks_of(2, groups)):
        send_rows(2, k, first, size)
    interpolate(0, range(len(chunks_of(0, groups))))
    write(0, 0, groups)
    write(1, 0, groups)

    def pack_edges(h, carry):
        to_right, to_left = carry
        for n in range(8):
            i = 8 * h + n
            turned = pltpu.roll(u[pl.ds(i * u_step, levels), :], i + 1, 1)
            to_right = jnp.where(lane == i, turned, to_right)
            to_left = jnp.where(lane == i + 1, turned, to_left)
        return to_right, to_left

    nothing = jnp.zeros((levels, COLS), F32)
    to_right, to_left = lax.fori_loop(0, ROWS // 8, pack_edges, (nothing, nothing))
    edge_right[...] = to_right
    edge_left[...] = pltpu.roll(to_left, ROWS - 1, 1)
    v_first[...] = v[u_step : u_step + levels]
    v_last[...] = v[ROWS * u_step : ROWS * u_step + levels]
    edges = [
        send(edge_right, u_west, (a, right)),
        send(edge_left, u_east, (a, left)),
        send(v_last, v_low, (up, s)),
        send(v_first, v_high, (down, s)),
    ]
    count = len(chunks_of(1, groups))
    interpolate(1, range(count - 1))
    interpolate(1, range(count - 1, count))
    interpolate(2, range(4))
    for copy in edges:
        copy.wait_recv()

    v[0:levels] = jnp.where(a == 0, 0.0, v_low[...])
    v[(ROWS + 1) * u_step : (ROWS + 1) * u_step + levels] = jnp.where(
        a == bands - 1, 0.0, v_high[...]
    )
    u_edges[...] = jnp.where(lane < ROWS, u_west[...], u_east[...])

    def diverge(h, carry):
        changes = []
        for m in range(4):
            blocks = []
            for n in range(4):
                i = 16 * h + 4 * m + n
                mine = (lane == i) | (lane == i + ROWS)
                blocks.append(
                    jnp.concatenate(
                        [u[pl.ds(i * u_step, levels), :], jnp.where(mine, u_edges[...], 0.0)], 1
                    )
                )
            changes.append(
                jnp.dot(
                    jnp.concatenate(blocks, 0).astype(BF16), slope[...], preferred_element_type=F32
                )
            )
        for m in range(4):
            for n in range(4):
                i = 16 * h + 4 * m + n
                south = v[pl.ds(i * u_step, levels), :]
                north = v[pl.ds((i + 2) * u_step, levels), :]
                rhs[pl.ds(i * rhs_step + 2 * levels, levels), :] = (
                    changes[m][n * levels : (n + 1) * levels] + 0.5 * (north - south)
                )
        return carry

    lax.fori_loop(0, ROWS // 16, diverge, 0)

    def solve(h, carry):
        for m in range(8):
            i = 16 * h + 2 * m
            both = jnp.concatenate(
                [
                    rhs[pl.ds(i * rhs_step, 3 * levels), :],
                    rhs[pl.ds((i + 1) * rhs_step, 3 * levels), :],
                ],
                1,
            ).astype(BF16)
            answer = jnp.dot(acoustic[...], both, preferred_element_type=F32)
            for c in range(0, 2 * levels, 8):
                at = c * solved_step + i
                solved[pl.ds(at, 8, stride=solved_step), :] = answer[c : c + 8, :COLS]
                solved[pl.ds(at + 1, 8, stride=solved_step), :] = answer[c : c + 8, COLS:]
        return carry

    lax.fori_loop(0, ROWS // 16, solve, 0)

    def round_off(g, carry):
        for q in range(GROUP):
            l = g * GROUP + q
            out[2, l] = solved[pl.ds(l * solved_step, ROWS), :].astype(BF16)
            out[5, l] = solved[pl.ds((l + levels) * solved_step, ROWS), :].astype(BF16)
        return carry

    lax.fori_loop(0, groups, round_off, 0)
    write(2, 0, groups)
    write(5, 0, groups)

    interpolate(2, range(4, len(chunks_of(2, groups))))
    for copy in sent:
        copy.wait_send()
    for copy in writes:
        copy.wait()


def hand_over(src, dst, held, in_sem, out_sem):
    size = src.shape[1] // PIECES
    pieces = [(f, pl.ds(n * size, size)) for f in range(6) for n in range(PIECES)]
    reads = [
        pltpu.make_async_copy(src.at[f, span], held.at[f, span], in_sem.at[k])
        for k, (f, span) in enumerate(pieces)
    ]
    writes = [
        pltpu.make_async_copy(held.at[f, span], dst.at[f, span], out_sem.at[k])
        for k, (f, span) in enumerate(pieces)
    ]
    for copy in reads:
        copy.start()
    for read, copy in zip(reads, writes):
        read.wait()
        copy.start()
    for copy in writes:
        copy.wait()


def local(bands, sectors, fields, frac_lat, off_lat, frac_lon, off_lon, sound_coef, inverse):
    levels = fields.shape[1]
    groups = levels // GROUP
    doubles = (groups + 1) // 2
    outside = pl.BlockSpec(memory_space=pltpu.HBM)
    halo_rows = pltpu.VMEM((3, levels, 16, COLS), BF16)
    halo_columns = pltpu.VMEM((3, doubles, 2 * ROWS, COLS), BF16)
    corners = pltpu.VMEM((4, 3, doubles, 16, COLS), BF16)
    level_rows = pltpu.VMEM((levels, COLS), F32)
    messages = 2 * sum(len(chunks_of(p, groups)) for p in range(3)) + 18 + 4
    outgoing = 4 + 2 * len(chunks_of(2, groups))
    stepped = pl.pallas_call(
        functools.partial(kernel, levels, bands, sectors),
        out_shape=jax.ShapeDtypeStruct(fields.shape, BF16),
        in_specs=[outside] * 7,
        out_specs=outside,
        scratch_shapes=[
            pltpu.VMEM(fields.shape, BF16),
            pltpu.VMEM(fields.shape, BF16),
            pltpu.VMEM((ROWS, levels), F32),
            pltpu.VMEM((ROWS, levels), jnp.int32),
            pltpu.VMEM((levels, COLS), F32),
            pltpu.VMEM((levels, COLS), jnp.int32),
            pltpu.VMEM((1, levels), F32),
            pltpu.VMEM((2 * levels, 2 * levels), F32),
            pltpu.VMEM((levels, ROWS), F32),
            pltpu.VMEM((levels, ROWS), jnp.int32),
            halo_rows, halo_rows, halo_rows, halo_rows,
            pltpu.VMEM((8, 2 * COLS, 2 * COLS), BF16),
            pltpu.VMEM((3, doubles, 2 * ROWS, 2 * COLS), F32),
            halo_columns, halo_columns, halo_columns, halo_columns,
            corners, corners,
            pltpu.VMEM((3, 2 * doubles, 2, ROWS + 2 * HALO, COLS), BF16),
            pltpu.VMEM((4, levels // 4, COLS), F32),
            pltpu.VMEM((levels // 4, COLS), jnp.int32),
            pltpu.VMEM((levels, ROWS, ROWS + 2 * HALO), BF16),
            pltpu.VMEM((4, levels, COLS), F32),
            level_rows,
            pltpu.VMEM((levels, 2 * COLS, COLS), BF16),
            pltpu.VMEM((GROUP, 2 * ROWS, 2 * COLS), BF16),
            pltpu.VMEM((ROWS * (levels + 1), COLS), F32),
            pltpu.VMEM(((ROWS + 2) * (levels + 1), COLS), F32),
        ]
        + [level_rows] * 9
        + [
            pltpu.VMEM((ROWS * (3 * levels + 1), COLS), F32),
            pltpu.VMEM((2 * levels * (ROWS + 1), COLS), F32),
            pltpu.VMEM((2 * levels, 3 * levels), BF16),
            pltpu.VMEM((2 * COLS, COLS), BF16),
            pltpu.SemaphoreType.DMA((4 + 2 * len(chunks_of(0, groups)) + 6,)),
            pltpu.SemaphoreType.DMA((outgoing,)),
            pltpu.SemaphoreType.DMA((messages,)),
            pltpu.SemaphoreType.DMA((messages,)),
        ],
        compiler_params=pltpu.CompilerParams(
            collective_id=0, has_side_effects=True, vmem_limit_bytes=60 * 2**20
        ),
        cost_estimate=pl.CostEstimate(
            flops=10**9, bytes_accessed=2 * 2 * fields.size, transcendentals=0
        ),
    )(
        fields, frac_lat[:, 0, :].T, off_lat[:, 0, :].T, frac_lon, off_lon,
        sound_coef[None, :], inverse,
    )
    return pl.pallas_call(
        hand_over,
        out_shape=jax.ShapeDtypeStruct(fields.shape, BF16),
        in_specs=[outside],
        out_specs=outside,
        scratch_shapes=[
            pltpu.VMEM(fields.shape, BF16),
            pltpu.SemaphoreType.DMA((6 * PIECES,)),
            pltpu.SemaphoreType.DMA((6 * PIECES,)),
        ],
        compiler_params=pltpu.CompilerParams(vmem_limit_bytes=60 * 2**20),
    )(stepped)


def solution(mesh):
    placed = (
        P(None, None, "lat", "lon"),
        P(None, "lon", "lat"),
        P(None, "lon", "lat"),
        P(None, "lat", "lon"),
        P(None, "lat", "lon"),
        P(),
        P(),
    )
    return jax.shard_map(
        functools.partial(local, mesh.shape["lat"], mesh.shape["lon"]),
        mesh=mesh, in_specs=placed, out_specs=P(None, None, "lat", "lon"), check_vma=False,
    )
```
